512 devices in a mesh: sib: 2 (over x_hi), row: 16 (over z, core), col: 16 (over y, x_lo).
Axes of the slice: x: 4 (x_hi: 2, x_lo: 2; x = x_hi * 2 + x_lo), y: 8, z: 8, core: 2. Of those that a mesh axis runs over, the one named last changes fastest.
Arguments:
- children: bfloat16 [2, 16384, 16384], P('sib', 'row', 'col'), as said below
- block_map: int32 [2, 128], P('sib'), may hold values from 0 to 127, as said below
- inverse_factor: bfloat16 [512, 512], replicated, as said below
Outputs:
- updated: float32 [16384, 16384], P('row', ('sib', 'col'))
The draws below stay inside these ranges and needn't reach their ends.
Inputs may be any that keep to these rules, and one draw needn't show every extreme that they name: `block_map`: each child's row is a permutation of 0 to 127, and it orders rows and columns alike. Of each aligned run of 8 child blocks, exactly 1 or none go to each aligned run of 8 parent blocks, and at most 1 go to each set of parent blocks p that agree in (p // 4) modulo the number of row groups. `children`: each child's contribution is symmetric. `inverse_factor`: lower triangular with a positive diagonal.
All inputs are finite; a program needn't handle non-finite values.
Results may differ from the reference program's by a relative error of at most 0.0035.
Values may be sent and summed in bfloat16 or wider, within the bound.
No kernel may reach another device: no remote copies, remote signals or barrier semaphores. Data moves between devices by JAX's collectives and lax.ppermute only.
A program may use at most 64 MiB of HBM per device.

```python
import math
import jax
import jax.numpy as jnp
from jax import lax

ORDER = 16384
BLOCK = 128
PANEL = 512
BLOCKS = 128
N_ROW = 16


def draw_children(key, part):
    key = jax.random.fold_in(key, 5)
    base = jax.random.normal(key, (2, ORDER, ORDER), jnp.float32)
    return ((base + jnp.swapaxes(base, 1, 2)) * 0.70710678).astype(jnp.bfloat16)


def draw_block_map(key, part):
    key = jax.random.fold_in(key, 3)
    groups = N_ROW
    width = BLOCKS // groups
    used = min(width, groups // 2)
    capacity = width // used

    def one_child(child_key):
        keys = jax.random.split(child_key, 4)
        residues = jax.random.permutation(keys[0], groups // 2)[:used]
        flips = jax.random.randint(keys[1], (used,), 0, 2)
        offsets = residues + groups // 2 * flips
        arrivals = jax.vmap(lambda k: jax.random.permutation(k, width))(jax.random.split(keys[2], groups))
        orders = jax.vmap(lambda k: jax.random.permutation(k, width))(jax.random.split(keys[3], groups))
        source = jnp.arange(groups, dtype=jnp.int32)[:, None]
        lane = orders // capacity
        target = (source + offsets[lane]) % groups
        place = arrivals[target, orders]
        return (target * width + place).reshape(-1).astype(jnp.int32)
    child_keys = jax.random.split(key, 2)
    return jnp.stack([one_child(child_keys[0]), one_child(child_keys[1])])


def draw_inverse_factor(key, part):
    key = jax.random.fold_in(key, 7)
    first, second = jax.random.split(key)
    lower = jax.random.normal(first, (PANEL, PANEL), jnp.float32) * (0.1 / math.sqrt(PANEL))
    diagonal = jax.random.uniform(second, (PANEL,), jnp.float32, 0.1, 0.15)
    rows_index = jnp.arange(PANEL)[:, None]
    cols_index = jnp.arange(PANEL)[None, :]
    result = jnp.where(cols_index < rows_index, lower, 0.0) + jnp.where(cols_index == rows_index, diagonal[:, None], 0.0)
    return result.astype(jnp.bfloat16)


def setup_inputs(seed: int = 0) -> dict:
    streams_of = jax.random.split(jax.random.key(seed), 4)
    return {
        "children": draw_children(jax.random.fold_in(streams_of[3], 71), 0),
        "block_map": draw_block_map(jax.random.fold_in(streams_of[3], 71), 0),
        "inverse_factor": draw_inverse_factor(jax.random.fold_in(streams_of[3], 71), 0),
    }


def element_order(row_map):
    inverse = jnp.argsort(row_map).astype(jnp.int32)
    inner = jnp.arange(BLOCK, dtype=jnp.int32)
    return (inverse[:, None] * BLOCK + inner[None, :]).reshape(-1)


def reference(children, block_map, inverse_factor):
    first_order = element_order(block_map[0])
    second_order = element_order(block_map[1])
    first_child = children[0]
    second_child = children[1]
    panel_front = (first_child[first_order][:, first_order[:PANEL]].astype(jnp.float32)
                   + second_child[second_order][:, second_order[:PANEL]].astype(jnp.float32))
    panel_input = panel_front.astype(jnp.bfloat16)
    panel_factor = jnp.dot(panel_input, inverse_factor.T, preferred_element_type=jnp.float32).astype(jnp.bfloat16)
    stride = ORDER // 16

    def one_band(band):
        start = band * stride
        first_rows = lax.dynamic_slice(first_order, (start,), (stride,))
        second_rows = lax.dynamic_slice(second_order, (start,), (stride,))
        front_band = (first_child[first_rows][:, first_order].astype(jnp.float32)
                      + second_child[second_rows][:, second_order].astype(jnp.float32))
        factor_band = lax.dynamic_slice_in_dim(panel_factor, start, stride, 0)
        return front_band - jnp.dot(factor_band, panel_factor.T, preferred_element_type=jnp.float32)

    bands = lax.map(one_band, jnp.arange(16, dtype=jnp.int32))
    return bands.reshape(ORDER, ORDER)
```

```python
import jax
import jax.numpy as jnp
from jax import lax
from jax.experimental import pallas as pl
from jax.experimental.pallas import tpu as pltpu
from jax.sharding import PartitionSpec as P

B = 128
H = B // 2
W = 8
G = 16
PANEL = 512
SMEM = pl.BlockSpec(memory_space=pltpu.SMEM)
ANY = pl.BlockSpec(memory_space=pl.ANY)
VMEM_LIMIT = 40 * 1024 * 1024


def params(flops=0, moved=0):
    return dict(
        compiler_params=pltpu.CompilerParams(vmem_limit_bytes=VMEM_LIMIT),
        cost_estimate=pl.CostEstimate(flops=flops, bytes_accessed=moved, transcendentals=0),
    )


def bf16(*shape):
    return jax.ShapeDtypeStruct(shape, jnp.bfloat16)


def ring(core, distance):
    return lax.bitwise_and(jnp.where(core == 0, distance, -distance), 7)


def row_slot(map_ref, q):
    row = lax.axis_index("row")
    target = map_ref[row * W + q] // W
    core = target % 2
    return lax.bitwise_xor(core, row % 2), ring(core, target // 2 - row // 2)


def row_landing(inv_ref, i):
    row = lax.axis_index("row")
    source = inv_ref[row * W + i] // W
    return lax.bitwise_xor(source % 2, row % 2), ring(row % 2, row // 2 - source // 2)


def col_slot(map_ref, v):
    return (map_ref[lax.axis_index("col") * W + v] // (W // 2)) % G


def col_landing(inv_ref, half, j):
    return inv_ref[(half * G + lax.axis_index("col")) * (W // 2) + j] // W


def lanes(j):
    return pl.ds(pl.multiple_of(j * B, B), B)


def pack(map_ref, tile, a, ob, sem_a, sem_b):
    for v in range(W):
        pltpu.make_async_copy(tile.at[:, pl.ds(0, H), pl.ds(v * B, B)], a.at[col_slot(map_ref, v)], sem_a).start()
    for q in range(W):
        e, k = row_slot(map_ref, q)
        pltpu.make_async_copy(tile.at[q, pl.ds(H, H), :], ob.at[e, k], sem_b).start()
    pltpu.make_async_copy(a.at[pl.ds(0, W)], a.at[pl.ds(0, W)], sem_a).wait()
    pltpu.make_async_copy(ob.at[0], ob.at[0], sem_b).wait()


def cols_to_rows(map_ref, inv_ref, arrived, ob, sem):
    @pl.loop(0, W)
    def _(q):
        e, k = row_slot(map_ref, q)
        for j in range(W):
            pltpu.make_async_copy(
                arrived.at[col_landing(inv_ref, j // 4, j % 4), q], ob.at[e, k, :, pl.ds(j * B, B)], sem
            ).start()
    pltpu.make_async_copy(ob.at[0], ob.at[0], sem).wait()


def rows_to_cols(map_ref, inv_ref, *refs):
    arrived, a, sem = refs[:8], refs[8], refs[9]

    @pl.loop(0, W)
    def _(i):
        e, k = row_landing(inv_ref, i)
        for step in range(8):
            @pl.when(k == step)
            def _():
                for v in range(W):
                    pltpu.make_async_copy(
                        arrived[step].at[e, :, pl.ds(v * B, B)], a.at[col_slot(map_ref, v), i], sem
                    ).start()
    pltpu.make_async_copy(a.at[pl.ds(0, W)], a.at[pl.ds(0, W)], sem).wait()


def split_rows(inv_ref, *refs):
    arrived, hand, kept, sem_h, sem_k = refs[:8], refs[8], refs[9], refs[10], refs[11]
    sib = lax.axis_index("sib")
    mine = pl.ds(pl.multiple_of(sib * PANEL, PANEL), PANEL)
    other = pl.ds(pl.multiple_of((1 - sib) * PANEL, PANEL), PANEL)

    @pl.loop(0, W)
    def _(i):
        e, k = row_landing(inv_ref, i)
        for step in range(8):
            @pl.when(k == step)
            def _():
                pltpu.make_async_copy(arrived[step].at[e, :, other], hand.at[i], sem_h).start()
                pltpu.make_async_copy(arrived[step].at[e, :, mine], kept.at[i], sem_k).start()
    pltpu.make_async_copy(hand, hand, sem_h).wait()
    pltpu.make_async_copy(kept, kept, sem_k).wait()


def split_cols(inv_ref, arrived, hand, kept, sem_h, sem_k):
    sib = lax.axis_index("sib")
    for j in range(W // 2):
        place = pl.ds(j * B, B)
        pltpu.make_async_copy(arrived.at[col_landing(inv_ref, 1 - sib, j)], hand.at[:, :, place], sem_h).start()
        pltpu.make_async_copy(arrived.at[col_landing(inv_ref, sib, j)], kept.at[:, :, place], sem_k).start()
    pltpu.make_async_copy(hand, hand, sem_h).wait()
    pltpu.make_async_copy(kept, kept, sem_k).wait()


def update(kept_a, kept_b, got_a, got_b, rows, cols, out):
    product = lax.dot_general(rows[...], cols[...], (((1,), (1,)), ((), ())), preferred_element_type=jnp.float32)
    f32 = jnp.float32
    out[0, 0:H] = kept_a[0].astype(f32) + got_a[0].astype(f32) - product[0:H]
    out[0, H:B] = kept_b[0].astype(f32) + got_b[0].astype(f32) - product[H:B]


def rows_permute(ob):
    other = lax.ppermute(ob[1], "row", [(i, i ^ 1) for i in range(G)])
    both = [jnp.stack([ob[0, k], other[k]]) for k in range(8)]
    arrived = [both[0]]
    for k in range(1, 8):
        pairs = [(z * 2 + c, (z + (k if c == 0 else -k)) % 8 * 2 + c) for z in range(8) for c in range(2)]
        arrived.append(lax.ppermute(both[k], "row", pairs))
    return arrived


def panel_piece(tile, maps, inv):
    row, col = lax.axis_index("row"), lax.axis_index("col")
    mine = lax.dynamic_slice_in_dim(maps, col * W, W, 0)
    owned = jnp.sum(jnp.where(mine < 4, jnp.arange(W, dtype=jnp.int32), 0))
    column = lax.dynamic_slice(tile, (0, owned * B), (W * B, B))
    out = jnp.transpose(column.reshape(W, G, 8, B), (1, 0, 2, 3))
    got = lax.all_to_all(out, "col", 0, 0, tiled=True)
    got = jnp.transpose(jnp.take(got, inv[:4] // W, axis=0, mode="clip"), (1, 0, 2, 3))
    targets = lax.dynamic_slice_in_dim(maps, row * W, W, 0) // W
    match = targets[None, :] == jnp.arange(G, dtype=jnp.int32)[:, None]
    source = jnp.sum(jnp.where(match, jnp.arange(W, dtype=jnp.int32)[None, :], 0), axis=1)
    got = lax.all_to_all(jnp.take(got, source, axis=0, mode="clip"), "row", 0, 0, tiled=True)
    landing = lax.dynamic_slice_in_dim(inv, row * W, W, 0) // W
    got = jnp.transpose(jnp.take(got, landing, axis=0, mode="clip"), (0, 2, 1, 3)).reshape(W * 8, PANEL)
    partner = lax.ppermute(got, "sib", [(0, 1), (1, 0)])
    return (got.astype(jnp.float32) + partner.astype(jnp.float32)).astype(jnp.bfloat16)


def panel_parts(piece):
    rows = lax.all_gather(piece, "col", axis=0, tiled=True)
    rows = jnp.transpose(rows.reshape(G, W, 8, PANEL), (1, 0, 2, 3)).reshape(W * B, PANEL)
    sib, row = lax.axis_index("sib"), lax.axis_index("row")
    half = jnp.where(sib == row // 8, 0, 1)
    send = lax.dynamic_slice_in_dim(piece, half * (W * 4), W * 4, 0)
    pairs = []
    for s in range(2):
        for g in range(G):
            for c in range(G):
                x = 0 if s == g // 8 else 1
                pairs.append((s * 256 + g * G + c, (g // 8) * 256 + c * G + (g % 8) * 2 + x))
    got = lax.ppermute(send, ("sib", "row", "col"), pairs)
    cols = lax.all_gather(got, "row", axis=0, tiled=True)
    cols = jnp.transpose(cols.reshape(G, W // 2, 8, PANEL), (1, 0, 2, 3)).reshape(PANEL, PANEL)
    return rows, cols


def factor(panel, inverse_factor):
    return lax.dot_general(
        panel, inverse_factor, (((1,), (1,)), ((), ())), preferred_element_type=jnp.float32
    ).astype(jnp.bfloat16)


def shards(children, block_map, inverse_factor):
    tile = children[0]
    maps = block_map[0]
    blocks = jnp.arange(maps.shape[0], dtype=jnp.int32)
    inv = jnp.sum(jnp.where(maps[None, :] == blocks[:, None], blocks[None, :], 0), axis=1)
    dma = pltpu.SemaphoreType.DMA
    MiB = 1 << 20

    slots, rows = bf16(G, W, H, B), bf16(2, 8, H, W * B)
    half = bf16(W, H, PANEL)
    send_a, send_b = pl.pallas_call(
        pack, out_shape=(slots, rows), in_specs=[SMEM, ANY], out_specs=(ANY, ANY), scratch_shapes=[dma, dma],
        **params(moved=4 * MiB),
    )(maps, tile.reshape(W, B, W * B))

    piece = panel_piece(tile, maps, inv)

    got_a = lax.all_to_all(send_a, "col", 0, 0, tiled=True)
    got_b = rows_permute(send_b)

    panel_rows, panel_cols = panel_parts(piece)

    send_a = pl.pallas_call(
        cols_to_rows, out_shape=rows, in_specs=[SMEM, SMEM, ANY], out_specs=ANY, scratch_shapes=[dma],
        **params(moved=2 * MiB),
    )(maps, inv, got_a)
    send_b = pl.pallas_call(
        rows_to_cols, out_shape=slots, in_specs=[SMEM, SMEM] + [ANY] * 8, out_specs=ANY, scratch_shapes=[dma],
        **params(moved=2 * MiB),
    )(maps, inv, *got_b)

    got_a = rows_permute(send_a)
    got_b = lax.all_to_all(send_b, "col", 0, 0, tiled=True)

    hand_a, kept_a = pl.pallas_call(
        split_rows, out_shape=(half, half), in_specs=[SMEM] + [ANY] * 8, out_specs=(ANY, ANY), scratch_shapes=[dma, dma],
        **params(moved=2 * MiB),
    )(inv, *got_a)
    hand_b, kept_b = pl.pallas_call(
        split_cols, out_shape=(half, half), in_specs=[SMEM, ANY], out_specs=(ANY, ANY), scratch_shapes=[dma, dma],
        **params(moved=2 * MiB),
    )(inv, got_b)
    swap = [(0, 1), (1, 0)]
    hand_a = lax.ppermute(hand_a, "sib", swap)
    hand_b = lax.ppermute(hand_b, "sib", swap)

    factor_rows = factor(panel_rows, inverse_factor)
    factor_cols = factor(panel_cols, inverse_factor)
    piece_spec = pl.BlockSpec((1, H, PANEL), lambda i: (i, 0, 0))
    out = pl.pallas_call(
        update, grid=(W,), out_shape=jax.ShapeDtypeStruct((W, B, PANEL), jnp.float32),
        in_specs=[piece_spec] * 4 + [
            pl.BlockSpec((B, PANEL), lambda i: (i, 0)), pl.BlockSpec((PANEL, PANEL), lambda i: (0, 0))],
        out_specs=pl.BlockSpec((1, B, PANEL), lambda i: (i, 0, 0)),
        **params(flops=2 * W * B * PANEL * PANEL, moved=6 * MiB),
    )(kept_a, kept_b, hand_a, hand_b, factor_rows, factor_cols)
    return out.reshape(W * B, PANEL)


def solution(mesh):
    in_specs = (P("sib", "row", "col"), P("sib", None), P())
    out_specs = P("row", ("sib", "col"))
    return jax.shard_map(shards, mesh=mesh, in_specs=in_specs, out_specs=out_specs, check_vma=False)
```

```python
import jax
import jax.numpy as jnp
from jax import lax
from jax.experimental import pallas as pl
from jax.experimental.pallas import tpu as pltpu
from jax.sharding import PartitionSpec as P

B = 128
HA = 64
HB = B - HA
W = 8
G = 16
PANEL = 512
TAIL = 16
SMEM = pl.BlockSpec(memory_space=pltpu.SMEM)
ANY = pl.BlockSpec(memory_space=pl.ANY)
VMEM = pl.BlockSpec(memory_space=pltpu.VMEM)
VMEM_LIMIT = 40 * 1024 * 1024


def params(flops=0, moved=0):
    return dict(
        compiler_params=pltpu.CompilerParams(vmem_limit_bytes=VMEM_LIMIT),
        cost_estimate=pl.CostEstimate(flops=flops, bytes_accessed=moved, transcendentals=0),
    )


def bf16(*shape):
    return jax.ShapeDtypeStruct(shape, jnp.bfloat16)


def ring(core, distance):
    return lax.bitwise_and(jnp.where(core == 0, distance, -distance), 7)


def row_slot(map_ref, q):
    row = lax.axis_index("row")
    target = map_ref[row * W + q] // W
    core = target % 2
    return lax.bitwise_xor(core, row % 2), ring(core, target // 2 - row // 2)


def row_landing(inv_ref, i):
    row = lax.axis_index("row")
    source = inv_ref[row * W + i] // W
    return lax.bitwise_xor(source % 2, row % 2), ring(row % 2, row // 2 - source // 2)


def col_slot(map_ref, v):
    return (map_ref[lax.axis_index("col") * W + v] // (W // 2)) % G


def col_landing(inv_ref, half, j):
    return inv_ref[(half * G + lax.axis_index("col")) * (W // 2) + j] // W


def lanes(j):
    return pl.ds(pl.multiple_of(j * B, B), B)


def pack(map_ref, tile, column, a, own, swap, sem_a, sem_b, sem_c):
    for v in range(W):
        pltpu.make_async_copy(
            tile.at[:, pl.ds(0, HA), pl.ds(v * B, B)], a.at[col_slot(map_ref, v), pl.ds(0, W)], sem_a
        ).start()
    sixteenths = pltpu.make_async_copy(column, a.at[:, W], sem_c)
    sixteenths.start()
    for q in range(W):
        e, k = row_slot(map_ref, q)
        for side, ob in enumerate((own, swap)):
            @pl.when(e == side)
            def _():
                pltpu.make_async_copy(tile.at[q, pl.ds(HA, HB), :], ob.at[k], sem_b).start()
    done = a.at[pl.ds(0, W), pl.ds(0, W)]
    pltpu.make_async_copy(done, done, sem_a).wait()
    pltpu.make_async_copy(own, own, sem_b).wait()
    sixteenths.wait()


def cols_to_rows(map_ref, map2_ref, inv_ref, arrived, taken, tail, own, swap, sem, sem_t):
    sib = lax.axis_index("sib")

    @pl.loop(0, W)
    def _(q):
        e, k = row_slot(map_ref, q)
        e2, k2 = row_slot(map2_ref, q)
        for side, ob in enumerate((own, swap)):
            @pl.when(e == side)
            def _():
                for j in range(W // 2):
                    pltpu.make_async_copy(
                        arrived.at[col_landing(inv_ref, sib, j), q],
                        ob.at[k, pl.ds(0, HA), pl.ds(j * B, B)], sem
                    ).start()

            @pl.when(e2 == side)
            def _():
                pltpu.make_async_copy(taken.at[q], ob.at[k2, pl.ds(0, HA), pl.ds(PANEL, PANEL)], sem).start()
            pltpu.make_async_copy(tail, ob.at[q, pl.ds(HA, TAIL), :], sem_t).start()
    done = own.at[:, pl.ds(0, HA), :]
    pltpu.make_async_copy(done, done, sem).wait()
    for ob in (own, swap):
        done = ob.at[:, pl.ds(HA, TAIL), :]
        pltpu.make_async_copy(done, done, sem_t).wait()


def rows_to_cols(map_ref, inv_ref, piece, *refs):
    arrived, a, sem, sem_p = refs[:8], refs[8], refs[9], refs[10]

    @pl.loop(0, W)
    def _(i):
        e, k = row_landing(inv_ref, i)
        for step in range(8):
            @pl.when(k == step)
            def _():
                for v in range(W):
                    pltpu.make_async_copy(
                        arrived[step].at[e, :, pl.ds(v * B, B)], a.at[col_slot(map_ref, v), i], sem
                    ).start()
    for t in range(G):
        pltpu.make_async_copy(piece, a.at[t, pl.ds(W, 4)], sem_p).start()
    done = a.at[pl.ds(0, W), pl.ds(0, W)]
    pltpu.make_async_copy(done, done, sem).wait()
    done = a.at[:, pl.ds(W, 4)]
    pltpu.make_async_copy(done, done, sem_p).wait()


def hand_cols(inv_ref, arrived, hand, sem):
    sib = lax.axis_index("sib")
    for j in range(W // 2):
        pltpu.make_async_copy(
            arrived.at[col_landing(inv_ref, 1 - sib, j), pl.ds(0, W)], hand.at[:, :, pl.ds(j * B, B)], sem
        ).start()
    pltpu.make_async_copy(hand, hand, sem).wait()


DIMS = (((1,), (1,)), ((), ()))


def factor_of(arrived, inverse, out, parts, panel, sem):
    copy = pltpu.make_async_copy(arrived.at[:, pl.ds(W, 4)], parts, sem)
    copy.start()
    copy.wait()
    for c in range(G):
        for j in range(4):
            part = parts[c, j].astype(jnp.float32)
            panel[:, c * 8:c * 8 + 8, j * B:j * B + B] = part.reshape(W, 8, B)

    @pl.loop(0, W)
    def _(p):
        out[pl.ds(pl.multiple_of(p * B, B), B), :] = lax.dot_general(
            panel[p].astype(jnp.bfloat16), inverse[...], DIMS, preferred_element_type=jnp.float32
        ).astype(jnp.bfloat16)


def keep(inv_ref, inv2_ref, *refs):
    arrived_a, refs = refs[:8], refs[8:]
    arrived_b, rows, inverse, base, kept_a, kept_b, pieces, panel, sem_a, sem_b, sem_p = refs
    sib, row = lax.axis_index("sib"), lax.axis_index("row")

    for step in range(8):
        z = lax.bitwise_and(row // 2 - jnp.where(row % 2 == 0, step, -step), 7)
        for e in range(2):
            origin = z * 2 + lax.bitwise_xor(row % 2, e)
            for h in range(2):
                pltpu.make_async_copy(
                    arrived_a[step].at[e, pl.ds(HA, TAIL), pl.ds(h * PANEL, PANEL)], pieces.at[origin, h], sem_p
                ).start()

    @pl.loop(0, W)
    def _(i):
        for child, ref in enumerate((inv_ref, inv2_ref)):
            e, k = row_landing(ref, i)
            for step in range(8):
                @pl.when(k == step)
                def _():
                    pltpu.make_async_copy(
                        arrived_a[step].at[e, pl.ds(0, HA), pl.ds(child * PANEL, PANEL)], kept_a.at[child, i], sem_a
                    ).start()
    for j in range(W // 2):
        pltpu.make_async_copy(
            arrived_b.at[col_landing(inv_ref, sib, j), pl.ds(0, W)], kept_b.at[:, :, pl.ds(j * B, B)], sem_b
        ).start()
    pltpu.make_async_copy(pieces, pieces, sem_p).wait()
    f32 = jnp.float32
    for p in range(W // 2):
        for r in range(G):
            low = (p % 2) * 8
            panel[p * B + r * 8:p * B + r * 8 + 8, :] = pieces[r, p // 2].astype(f32)[low:low + 8]
    cols = lax.dot_general(panel[...].astype(jnp.bfloat16), inverse[...], DIMS, preferred_element_type=f32)
    panel[...] = cols.astype(jnp.bfloat16).astype(f32)
    pltpu.make_async_copy(kept_a, kept_a, sem_a).wait()
    pltpu.make_async_copy(kept_b, kept_b, sem_b).wait()

    @pl.loop(0, W)
    def _(i):
        block = rows[pl.ds(pl.multiple_of(i * B, B), B), :]
        product = lax.dot_general(block, panel[...].astype(jnp.bfloat16), DIMS, preferred_element_type=f32)
        base[i, 0:HA] = kept_a[0, i].astype(f32) + kept_a[1, i].astype(f32) - product[0:HA]
        base[i, HA:B] = kept_b[i].astype(f32) - product[HA:B]


def join(base, got_b, out):
    out[:, 0:HA] = base[:, 0:HA]
    out[:, HA:B] = base[:, HA:B] + got_b[...].astype(jnp.float32)


def core_exchange(swap):
    return lax.ppermute(swap, "row", [(i, i ^ 1) for i in range(G)])


def pairs_of(own, other):
    return [jnp.stack([own[k], other[k]]) for k in range(8)]


def z_ring(both):
    arrived = [both[0]] + [None] * 7
    for k in (4, 3, 5, 2, 6, 1, 7):
        pairs = [(z * 2 + c, (z + (k if c == 0 else -k)) % 8 * 2 + c) for z in range(8) for c in range(2)]
        arrived[k] = lax.ppermute(both[k], "row", pairs)
    return arrived


def inverse_of(maps):
    blocks = jnp.arange(maps.shape[0], dtype=jnp.int32)
    return jnp.sum(jnp.where(maps[None, :] == blocks[:, None], blocks[None, :], 0), axis=1)


def panel_column(tile, maps):
    mine = lax.dynamic_slice_in_dim(maps, lax.axis_index("col") * W, W, 0)
    owned = jnp.sum(jnp.where(mine < 4, jnp.arange(W, dtype=jnp.int32), 0))
    column = lax.dynamic_slice(tile, (0, owned * B), (W * B, B))
    return jnp.transpose(column.reshape(W, G, 8, B), (1, 0, 2, 3)).reshape(G, W * 8, B)


def panel_piece(got, maps, inv, inv2, early):
    sib, row = lax.axis_index("sib"), lax.axis_index("row")
    got = jnp.transpose(jnp.take(got, inv[:4] // W, axis=0, mode="clip"), (1, 0, 2, 3))
    targets = lax.dynamic_slice_in_dim(maps, row * W, W, 0) // W
    match = targets[None, :] == (jnp.arange(2 * G, dtype=jnp.int32) % G)[:, None]
    source = jnp.sum(jnp.where(match, jnp.arange(W, dtype=jnp.int32)[None, :], 0), axis=1)
    got = lax.all_to_all(jnp.take(got, source, axis=0, mode="clip"), ("sib", "row"), 0, 0, tiled=True)
    got, early = lax.optimization_barrier((got, early))
    parts = [
        jnp.take(got, child * G + lax.dynamic_slice_in_dim(ref, row * W, W, 0) // W, axis=0, mode="clip").astype(jnp.float32)
        for child, ref in ((sib, inv), (1 - sib, inv2))
    ]
    return (parts[0] + parts[1]).astype(jnp.bfloat16), early


def tail_piece(piece):
    sib, row = lax.axis_index("sib"), lax.axis_index("row")
    half = jnp.where(sib == row // 8, 0, 1)
    send = lax.dynamic_slice_in_dim(jnp.transpose(piece, (0, 2, 1, 3)).reshape(W * 8, PANEL), half * (W * 4), W * 4, 0)
    pairs = []
    for s in range(2):
        for g in range(G):
            for c in range(G):
                x = 0 if s == g // 8 else 1
                pairs.append((s * 256 + g * G + c, (g // 8) * 256 + c * G + (g % 8) * 2 + x))
    got = lax.ppermute(send, ("sib", "row", "col"), pairs)
    return jnp.concatenate([got[:16], got[16:]], axis=1)


def shards(children, block_map, inverse_factor):
    tile = children[0]
    maps = block_map[0]
    dma = pltpu.SemaphoreType.DMA
    MiB = 1 << 20
    exchange = [(0, 1), (1, 0)]
    maps2 = lax.ppermute(maps, "sib", exchange)
    inv = inverse_of(maps)
    blocks = tile.reshape(W, B, W * B)

    rows_a, rows_b = bf16(8, HA + TAIL, W * B), bf16(8, HB, W * B)
    send_a, own, swap = pl.pallas_call(
        pack, out_shape=(bf16(G, W + 1, HA, B), rows_b, rows_b), in_specs=[SMEM, ANY, ANY], out_specs=(ANY, ANY, ANY),
        scratch_shapes=[dma, dma, dma], **params(moved=4 * MiB),
    )(maps, blocks, panel_column(tile, maps))
    got_a = lax.all_to_all(send_a, "col", 0, 0, tiled=True)
    got_b = z_ring(pairs_of(own, core_exchange(swap)))
    got_a, maps2, got_b[7], got_b[6], got_b[5], got_b[4], got_b[3] = lax.optimization_barrier(
        (got_a, maps2, got_b[7], got_b[6], got_b[5], got_b[4], got_b[3]))

    inv2 = inverse_of(maps2)
    hand_a = pl.pallas_call(
        hand_cols, out_shape=bf16(W, HA, PANEL), in_specs=[SMEM, ANY], out_specs=VMEM, scratch_shapes=[dma],
        **params(moved=MiB),
    )(inv, got_a)
    taken_a = lax.ppermute(hand_a, "sib", exchange)
    piece, taken_a = panel_piece(got_a[:, W].reshape(G, W, 8, B), maps, inv, inv2, taken_a)
    tail = tail_piece(piece)
    send_b = pl.pallas_call(
        rows_to_cols, out_shape=bf16(G, W + 4, HB, B), in_specs=[SMEM, SMEM] + [ANY] * 9, out_specs=ANY,
        scratch_shapes=[dma, dma], **params(moved=3 * MiB),
    )(maps, inv, jnp.transpose(piece, (1, 0, 2, 3)).reshape(4, W * 8, B), *got_b)
    send_b, tail = lax.optimization_barrier((send_b, tail))
    got_b = lax.all_to_all(send_b, "col", 0, 0, tiled=True)
    own, swap = pl.pallas_call(
        cols_to_rows, out_shape=(rows_a, rows_a), in_specs=[SMEM] * 3 + [ANY] * 3, out_specs=(ANY, ANY),
        scratch_shapes=[dma, dma], **params(moved=2 * MiB),
    )(maps, maps2, inv, got_a, taken_a, tail)
    got_a = z_ring(pairs_of(own, core_exchange(swap)))
    got_b, got_a = lax.optimization_barrier((got_b, got_a))

    hand_b = pl.pallas_call(
        hand_cols, out_shape=bf16(W, HB, PANEL), in_specs=[SMEM, ANY], out_specs=VMEM, scratch_shapes=[dma],
        **params(moved=MiB),
    )(inv, got_b)
    taken_b = lax.ppermute(hand_b, "sib", exchange)
    factor_rows = pl.pallas_call(
        factor_of, out_shape=bf16(W * B, PANEL), in_specs=[ANY, VMEM], out_specs=VMEM,
        scratch_shapes=[pltpu.VMEM((G, 4, W * 8, B), jnp.bfloat16), pltpu.VMEM((W, B, PANEL), jnp.float32), dma],
        **params(flops=2 * W * B * PANEL * PANEL, moved=2 * MiB),
    )(got_b, inverse_factor)
    full = jax.ShapeDtypeStruct((W, B, PANEL), jnp.float32)
    base = pl.pallas_call(
        keep, out_shape=full, in_specs=[SMEM] * 2 + [ANY] * 9 + [VMEM] * 2, out_specs=VMEM,
        scratch_shapes=[pltpu.VMEM((2, W, HA, PANEL), jnp.bfloat16), pltpu.VMEM((W, HB, PANEL), jnp.bfloat16),
                        pltpu.VMEM((G, 2, 16, PANEL), jnp.bfloat16), pltpu.VMEM((PANEL, PANEL), jnp.float32), dma, dma, dma],
        **params(flops=3 * W * B * PANEL * PANEL, moved=6 * MiB),
    )(inv, inv2, *got_a, got_b, factor_rows, inverse_factor)
    full_spec = pl.BlockSpec((2, B, PANEL), lambda i: (i, 0, 0))
    out = pl.pallas_call(
        join, grid=(W // 2,), out_shape=full, in_specs=[full_spec, pl.BlockSpec((2, HB, PANEL), lambda i: (i, 0, 0))],
        out_specs=full_spec, **params(moved=5 * MiB),
    )(base, taken_b)
    return out.reshape(W * B, PANEL)


def solution(mesh):
    in_specs = (P("sib", "row", "col"), P("sib", None), P())
    out_specs = P("row", ("sib", "col"))
    return jax.shard_map(shards, mesh=mesh, in_specs=in_specs, out_specs=out_specs, check_vma=False)
```

```python
import jax
import jax.numpy as jnp
from jax import lax
from jax.experimental import pallas as pl
from jax.experimental.pallas import tpu as pltpu
from jax.sharding import PartitionSpec as P

B = 128
HA = 64
HB = B - HA
W = 8
G = 16
PANEL = 512
TAIL = 16
SMEM = pl.BlockSpec(memory_space=pltpu.SMEM)
ANY = pl.BlockSpec(memory_space=pl.ANY)
VMEM = pl.BlockSpec(memory_space=pltpu.VMEM)
VMEM_LIMIT = 40 * 1024 * 1024


def params(flops=0, moved=0):
    return dict(
        compiler_params=pltpu.CompilerParams(vmem_limit_bytes=VMEM_LIMIT),
        cost_estimate=pl.CostEstimate(flops=flops, bytes_accessed=moved, transcendentals=0),
    )


def bf16(*shape):
    return jax.ShapeDtypeStruct(shape, jnp.bfloat16)


def ring(core, distance):
    return lax.bitwise_and(jnp.where(core == 0, distance, -distance), 7)


def row_slot(map_ref, q):
    row = lax.axis_index("row")
    target = map_ref[row * W + q] // W
    core = target % 2
    return lax.bitwise_xor(core, row % 2), ring(core, target // 2 - row // 2)


def row_landing(inv_ref, i):
    row = lax.axis_index("row")
    source = inv_ref[row * W + i] // W
    return lax.bitwise_xor(source % 2, row % 2), ring(row % 2, row // 2 - source // 2)


def col_slot(map_ref, v):
    return (map_ref[lax.axis_index("col") * W + v] // (W // 2)) % G


def col_landing(inv_ref, half, j):
    return inv_ref[(half * G + lax.axis_index("col")) * (W // 2) + j] // W


def lanes(j):
    return pl.ds(pl.multiple_of(j * B, B), B)


def pack_cols(map_ref, tile, column, a, sem_a, sem_c):
    for v in range(W):
        pltpu.make_async_copy(
            tile.at[:, pl.ds(0, HA), pl.ds(v * B, B)], a.at[col_slot(map_ref, v), pl.ds(0, W)], sem_a
        ).start()
    sixteenths = pltpu.make_async_copy(column, a.at[:, W], sem_c)
    sixteenths.start()
    done = a.at[pl.ds(0, W), pl.ds(0, W)]
    pltpu.make_async_copy(done, done, sem_a).wait()
    sixteenths.wait()


def pack_rows(map_ref, tile, own, swap, sem):
    for q in range(W):
        e, k = row_slot(map_ref, q)
        for side, ob in enumerate((own, swap)):
            @pl.when(e == side)
            def _():
                pltpu.make_async_copy(tile.at[q, pl.ds(HA, HB), :], ob.at[k], sem).start()
    pltpu.make_async_copy(own, own, sem).wait()


def cols_to_rows(map_ref, map2_ref, inv_ref, arrived, taken, tail, own, swap, sem, sem_t):
    sib = lax.axis_index("sib")

    @pl.loop(0, W)
    def _(q):
        e, k = row_slot(map_ref, q)
        e2, k2 = row_slot(map2_ref, q)
        for side, ob in enumerate((own, swap)):
            @pl.when(e == side)
            def _():
                for j in range(W // 2):
                    pltpu.make_async_copy(
                        arrived.at[col_landing(inv_ref, sib, j), q],
                        ob.at[k, pl.ds(0, HA), pl.ds(j * B, B)], sem
                    ).start()

            @pl.when(e2 == side)
            def _():
                pltpu.make_async_copy(taken.at[q], ob.at[k2, pl.ds(0, HA), pl.ds(PANEL, PANEL)], sem).start()
            pltpu.make_async_copy(tail, ob.at[q, pl.ds(HA, TAIL), :], sem_t).start()
    done = own.at[:, pl.ds(0, HA), :]
    pltpu.make_async_copy(done, done, sem).wait()
    for ob in (own, swap):
        done = ob.at[:, pl.ds(HA, TAIL), :]
        pltpu.make_async_copy(done, done, sem_t).wait()


def rows_to_cols(map_ref, inv_ref, *refs):
    arrived, a, sem = refs[:8], refs[8], refs[9]

    @pl.loop(0, W)
    def _(i):
        e, k = row_landing(inv_ref, i)
        for step in range(8):
            @pl.when(k == step)
            def _():
                for v in range(W):
                    pltpu.make_async_copy(
                        arrived[step].at[e, :, pl.ds(v * B, B)], a.at[col_slot(map_ref, v), i], sem
                    ).start()
    done = a.at[pl.ds(0, W), pl.ds(0, W)]
    pltpu.make_async_copy(done, done, sem).wait()


def add_piece(piece, a, filled, sem):
    for t in range(G):
        pltpu.make_async_copy(piece, filled.at[t, pl.ds(W, 4)], sem).start()
    done = filled.at[:, pl.ds(W, 4)]
    pltpu.make_async_copy(done, done, sem).wait()


def hand_cols(inv_ref, arrived, hand, sem):
    sib = lax.axis_index("sib")
    for j in range(W // 2):
        pltpu.make_async_copy(
            arrived.at[col_landing(inv_ref, 1 - sib, j), pl.ds(0, W)], hand.at[:, :, pl.ds(j * B, B)], sem
        ).start()
    pltpu.make_async_copy(hand, hand, sem).wait()


DIMS = (((1,), (1,)), ((), ()))


def factor_of(arrived, inverse, out, parts, panel, sem):
    copy = pltpu.make_async_copy(arrived.at[:, pl.ds(W, 4)], parts, sem)
    copy.start()
    copy.wait()
    for c in range(G):
        for j in range(4):
            part = parts[c, j].astype(jnp.float32)
            panel[:, c * 8:c * 8 + 8, j * B:j * B + B] = part.reshape(W, 8, B)

    @pl.loop(0, W)
    def _(p):
        out[pl.ds(pl.multiple_of(p * B, B), B), :] = lax.dot_general(
            panel[p].astype(jnp.bfloat16), inverse[...], DIMS, preferred_element_type=jnp.float32
        ).astype(jnp.bfloat16)


def keep(inv_ref, inv2_ref, *refs):
    arrived_a, refs = refs[:8], refs[8:]
    arrived_b, rows, inverse, base, kept_a, kept_b, pieces, panel, sem_a, sem_b, sem_p = refs
    sib, row = lax.axis_index("sib"), lax.axis_index("row")

    for step in range(8):
        z = lax.bitwise_and(row // 2 - jnp.where(row % 2 == 0, step, -step), 7)
        for e in range(2):
            origin = z * 2 + lax.bitwise_xor(row % 2, e)
            for h in range(2):
                pltpu.make_async_copy(
                    arrived_a[step].at[e, pl.ds(HA, TAIL), pl.ds(h * PANEL, PANEL)], pieces.at[origin, h], sem_p
                ).start()

    @pl.loop(0, W)
    def _(i):
        for child, ref in enumerate((inv_ref, inv2_ref)):
            e, k = row_landing(ref, i)
            for step in range(8):
                @pl.when(k == step)
                def _():
                    pltpu.make_async_copy(
                        arrived_a[step].at[e, pl.ds(0, HA), pl.ds(child * PANEL, PANEL)], kept_a.at[child, i], sem_a
                    ).start()
    for j in range(W // 2):
        pltpu.make_async_copy(
            arrived_b.at[col_landing(inv_ref, sib, j), pl.ds(0, W)], kept_b.at[:, :, pl.ds(j * B, B)], sem_b
        ).start()
    pltpu.make_async_copy(pieces, pieces, sem_p).wait()
    f32 = jnp.float32
    for p in range(W // 2):
        for r in range(G):
            low = (p % 2) * 8
            panel[p * B + r * 8:p * B + r * 8 + 8, :] = pieces[r, p // 2].astype(f32)[low:low + 8]
    cols = lax.dot_general(panel[...].astype(jnp.bfloat16), inverse[...], DIMS, preferred_element_type=f32)
    panel[...] = cols.astype(jnp.bfloat16).astype(f32)
    pltpu.make_async_copy(kept_a, kept_a, sem_a).wait()
    pltpu.make_async_copy(kept_b, kept_b, sem_b).wait()

    @pl.loop(0, W)
    def _(i):
        block = rows[pl.ds(pl.multiple_of(i * B, B), B), :]
        product = lax.dot_general(block, panel[...].astype(jnp.bfloat16), DIMS, preferred_element_type=f32)
        base[i, 0:HA] = kept_a[0, i].astype(f32) + kept_a[1, i].astype(f32) - product[0:HA]
        base[i, HA:B] = kept_b[i].astype(f32) - product[HA:B]


def join(base, got_b, out):
    out[:, 0:HA] = base[:, 0:HA]
    out[:, HA:B] = base[:, HA:B] + got_b[...].astype(jnp.float32)


def core_exchange(swap):
    return lax.ppermute(swap, "row", [(i, i ^ 1) for i in range(G)])


def pairs_of(own, other):
    return [jnp.stack([own[k], other[k]]) for k in range(8)]


def z_ring(both):
    arrived = [both[0]] + [None] * 7
    for k in (4, 3, 5, 2, 6, 1, 7):
        pairs = [(z * 2 + c, (z + (k if c == 0 else -k)) % 8 * 2 + c) for z in range(8) for c in range(2)]
        arrived[k] = lax.ppermute(both[k], "row", pairs)
    return arrived


def inverse_of(maps):
    blocks = jnp.arange(maps.shape[0], dtype=jnp.int32)
    return jnp.sum(jnp.where(maps[None, :] == blocks[:, None], blocks[None, :], 0), axis=1)


def panel_column(tile, maps):
    mine = lax.dynamic_slice_in_dim(maps, lax.axis_index("col") * W, W, 0)
    owned = jnp.sum(jnp.where(mine < 4, jnp.arange(W, dtype=jnp.int32), 0))
    column = lax.dynamic_slice(tile, (0, owned * B), (W * B, B))
    return jnp.transpose(column.reshape(W, G, 8, B), (1, 0, 2, 3)).reshape(G, W * 8, B)


def panel_slots(got, maps, inv):
    got = jnp.transpose(jnp.take(got, inv[:4] // W, axis=0, mode="clip"), (1, 0, 2, 3))
    targets = lax.dynamic_slice_in_dim(maps, lax.axis_index("row") * W, W, 0) // W
    match = targets[None, :] == (jnp.arange(2 * G, dtype=jnp.int32) % G)[:, None]
    source = jnp.sum(jnp.where(match, jnp.arange(W, dtype=jnp.int32)[None, :], 0), axis=1)
    return jnp.take(got, source, axis=0, mode="clip")


def panel_piece(got, inv, inv2):
    sib, row = lax.axis_index("sib"), lax.axis_index("row")
    parts = [
        jnp.take(got, child * G + lax.dynamic_slice_in_dim(ref, row * W, W, 0) // W, axis=0, mode="clip").astype(jnp.float32)
        for child, ref in ((sib, inv), (1 - sib, inv2))
    ]
    return (parts[0] + parts[1]).astype(jnp.bfloat16)


def tail_piece(piece):
    sib, row = lax.axis_index("sib"), lax.axis_index("row")
    half = jnp.where(sib == row // 8, 0, 1)
    send = lax.dynamic_slice_in_dim(jnp.transpose(piece, (0, 2, 1, 3)).reshape(W * 8, PANEL), half * (W * 4), W * 4, 0)
    pairs = []
    for s in range(2):
        for g in range(G):
            for c in range(G):
                x = 0 if s == g // 8 else 1
                pairs.append((s * 256 + g * G + c, (g // 8) * 256 + c * G + (g % 8) * 2 + x))
    got = lax.ppermute(send, ("sib", "row", "col"), pairs)
    return jnp.concatenate([got[:16], got[16:]], axis=1)


def shards(children, block_map, inverse_factor):
    tile = children[0]
    maps = block_map[0]
    dma = pltpu.SemaphoreType.DMA
    MiB = 1 << 20
    exchange = [(0, 1), (1, 0)]
    maps2 = lax.ppermute(maps, "sib", exchange)
    inv = inverse_of(maps)
    blocks = tile.reshape(W, B, W * B)

    rows_a, rows_b = bf16(8, HA + TAIL, W * B), bf16(8, HB, W * B)
    send_a = pl.pallas_call(
        pack_cols, out_shape=bf16(G, W + 1, HA, B), in_specs=[SMEM, ANY, ANY], out_specs=ANY,
        scratch_shapes=[dma, dma], **params(moved=2 * MiB),
    )(maps, blocks, panel_column(tile, maps))
    own, swap = pl.pallas_call(
        pack_rows, out_shape=(rows_b, rows_b), in_specs=[SMEM, ANY], out_specs=(ANY, ANY), scratch_shapes=[dma],
        **params(moved=2 * MiB),
    )(maps, blocks)
    got_a = lax.all_to_all(send_a, "col", 0, 0, tiled=True)
    got_b = z_ring(pairs_of(own, core_exchange(swap)))
    got_a, maps2, got_b[7], got_b[6], got_b[5] = lax.optimization_barrier(
        (got_a, maps2, got_b[7], got_b[6], got_b[5]))

    inv2 = inverse_of(maps2)
    pieces, got_a = lax.optimization_barrier((panel_slots(got_a[:, W].reshape(G, W, 8, B), maps, inv), got_a))
    hand_a = pl.pallas_call(
        hand_cols, out_shape=bf16(W, HA, PANEL), in_specs=[SMEM, ANY], out_specs=VMEM, scratch_shapes=[dma],
        **params(moved=MiB),
    )(inv, got_a)
    taken_a = lax.ppermute(hand_a, "sib", exchange)
    send_b = pl.pallas_call(
        rows_to_cols, out_shape=bf16(G, W + 4, HB, B), in_specs=[SMEM, SMEM] + [ANY] * 8, out_specs=ANY,
        scratch_shapes=[dma], **params(moved=2 * MiB),
    )(maps, inv, *got_b)
    pieces = lax.all_to_all(pieces, ("sib", "row"), 0, 0, tiled=True)
    pieces, taken_a, send_b = lax.optimization_barrier((pieces, taken_a, send_b))
    piece = panel_piece(pieces, inv, inv2)
    tail = tail_piece(piece)
    send_b = pl.pallas_call(
        add_piece, out_shape=bf16(G, W + 4, HB, B), in_specs=[ANY, ANY], out_specs=ANY, scratch_shapes=[dma],
        input_output_aliases={1: 0}, **params(moved=MiB),
    )(jnp.transpose(piece, (1, 0, 2, 3)).reshape(4, W * 8, B), send_b)
    send_b, tail = lax.optimization_barrier((send_b, tail))
    got_b = lax.all_to_all(send_b, "col", 0, 0, tiled=True)
    own, swap = pl.pallas_call(
        cols_to_rows, out_shape=(rows_a, rows_a), in_specs=[SMEM] * 3 + [ANY] * 3, out_specs=(ANY, ANY),
        scratch_shapes=[dma, dma], **params(moved=2 * MiB),
    )(maps, maps2, inv, got_a, taken_a, tail)
    got_a = z_ring(pairs_of(own, core_exchange(swap)))
    got_b, got_a = lax.optimization_barrier((got_b, got_a))

    hand_b = pl.pallas_call(
        hand_cols, out_shape=bf16(W, HB, PANEL), in_specs=[SMEM, ANY], out_specs=VMEM, scratch_shapes=[dma],
        **params(moved=MiB),
    )(inv, got_b)
    taken_b = lax.ppermute(hand_b, "sib", exchange)
    factor_rows = pl.pallas_call(
        factor_of, out_shape=bf16(W * B, PANEL), in_specs=[ANY, VMEM], out_specs=VMEM,
        scratch_shapes=[pltpu.VMEM((G, 4, W * 8, B), jnp.bfloat16), pltpu.VMEM((W, B, PANEL), jnp.float32), dma],
        **params(flops=2 * W * B * PANEL * PANEL, moved=2 * MiB),
    )(got_b, inverse_factor)
    full = jax.ShapeDtypeStruct((W, B, PANEL), jnp.float32)
    base = pl.pallas_call(
        keep, out_shape=full, in_specs=[SMEM] * 2 + [ANY] * 9 + [VMEM] * 2, out_specs=VMEM,
        scratch_shapes=[pltpu.VMEM((2, W, HA, PANEL), jnp.bfloat16), pltpu.VMEM((W, HB, PANEL), jnp.bfloat16),
                        pltpu.VMEM((G, 2, 16, PANEL), jnp.bfloat16), pltpu.VMEM((PANEL, PANEL), jnp.float32), dma, dma, dma],
        **params(flops=3 * W * B * PANEL * PANEL, moved=6 * MiB),
    )(inv, inv2, *got_a, got_b, factor_rows, inverse_factor)
    full_spec = pl.BlockSpec((2, B, PANEL), lambda i: (i, 0, 0))
    out = pl.pallas_call(
        join, grid=(W // 2,), out_shape=full, in_specs=[full_spec, pl.BlockSpec((2, HB, PANEL), lambda i: (i, 0, 0))],
        out_specs=full_spec, **params(moved=5 * MiB),
    )(base, taken_b)
    return out.reshape(W * B, PANEL)


def solution(mesh):
    in_specs = (P("sib", "row", "col"), P("sib", None), P())
    out_specs = P("row", ("sib", "col"))
    return jax.shard_map(shards, mesh=mesh, in_specs=in_specs, out_specs=out_specs, check_vma=False)
```

```python
import jax
import jax.numpy as jnp
from jax import lax
from jax.experimental import pallas as pl
from jax.experimental.pallas import tpu as pltpu
from jax.sharding import PartitionSpec as P

B = 128
HA = 64
HB = B - HA
W = 8
G = 16
PANEL = 512
TAIL = 16
SMEM = pl.BlockSpec(memory_space=pltpu.SMEM)
ANY = pl.BlockSpec(memory_space=pl.ANY)
VMEM = pl.BlockSpec(memory_space=pltpu.VMEM)
VMEM_LIMIT = 40 * 1024 * 1024


def params(flops=0, moved=0):
    return dict(
        compiler_params=pltpu.CompilerParams(vmem_limit_bytes=VMEM_LIMIT),
        cost_estimate=pl.CostEstimate(flops=flops, bytes_accessed=moved, transcendentals=0),
    )


def bf16(*shape):
    return jax.ShapeDtypeStruct(shape, jnp.bfloat16)


def ring(core, distance):
    return lax.bitwise_and(jnp.where(core == 0, distance, -distance), 7)


def row_slot(map_ref, q):
    row = lax.axis_index("row")
    target = map_ref[row * W + q] // W
    core = target % 2
    return lax.bitwise_xor(core, row % 2), ring(core, target // 2 - row // 2)


def row_landing(inv_ref, i):
    row = lax.axis_index("row")
    source = inv_ref[row * W + i] // W
    return lax.bitwise_xor(source % 2, row % 2), ring(row % 2, row // 2 - source // 2)


def col_slot(map_ref, v):
    return (map_ref[lax.axis_index("col") * W + v] // (W // 2)) % G


def col_landing(inv_ref, half, j):
    return inv_ref[(half * G + lax.axis_index("col")) * (W // 2) + j] // W


def lanes(j):
    return pl.ds(pl.multiple_of(j * B, B), B)


def pack_cols(map_ref, tile, column, a, sem_a, sem_c):
    for v in range(W):
        pltpu.make_async_copy(
            tile.at[:, pl.ds(0, HA), pl.ds(v * B, B)], a.at[col_slot(map_ref, v), pl.ds(0, W)], sem_a
        ).start()
    sixteenths = pltpu.make_async_copy(column, a.at[:, W], sem_c)
    sixteenths.start()
    done = a.at[pl.ds(0, W), pl.ds(0, W)]
    pltpu.make_async_copy(done, done, sem_a).wait()
    sixteenths.wait()


def pack_rows(map_ref, tile, own, swap, sem):
    for q in range(W):
        e, k = row_slot(map_ref, q)
        for side, ob in enumerate((own, swap)):
            @pl.when(e == side)
            def _():
                pltpu.make_async_copy(tile.at[q, pl.ds(HA, HB), :], ob.at[k], sem).start()
    pltpu.make_async_copy(own, own, sem).wait()


def cols_to_rows(map_ref, map2_ref, inv_ref, arrived, taken, own, swap, sem):
    sib = lax.axis_index("sib")

    @pl.loop(0, W)
    def _(q):
        e, k = row_slot(map_ref, q)
        e2, k2 = row_slot(map2_ref, q)
        for side, ob in enumerate((own, swap)):
            @pl.when(e == side)
            def _():
                for j in range(W // 2):
                    pltpu.make_async_copy(
                        arrived.at[col_landing(inv_ref, sib, j), q], ob.at[k, :, pl.ds(j * B, B)], sem
                    ).start()

            @pl.when(e2 == side)
            def _():
                pltpu.make_async_copy(taken.at[q], ob.at[k2, :, pl.ds(PANEL, PANEL)], sem).start()
    pltpu.make_async_copy(own, own, sem).wait()


def rows_to_cols(map_ref, inv_ref, *refs):
    arrived, a, sem = refs[:8], refs[8], refs[9]

    @pl.loop(0, W)
    def _(i):
        e, k = row_landing(inv_ref, i)
        for step in range(8):
            @pl.when(k == step)
            def _():
                for v in range(W):
                    pltpu.make_async_copy(
                        arrived[step].at[e, :, pl.ds(v * B, B)], a.at[col_slot(map_ref, v), i], sem
                    ).start()
    done = a.at[pl.ds(0, W), pl.ds(0, W)]
    pltpu.make_async_copy(done, done, sem).wait()


def add_piece(piece, a, filled, sem):
    for t in range(G):
        pltpu.make_async_copy(piece, filled.at[t, pl.ds(W, 4)], sem).start()
    done = filled.at[:, pl.ds(W, 4)]
    pltpu.make_async_copy(done, done, sem).wait()


def hand_cols(inv_ref, arrived, hand, sem):
    sib = lax.axis_index("sib")
    for j in range(W // 2):
        pltpu.make_async_copy(
            arrived.at[col_landing(inv_ref, 1 - sib, j), pl.ds(0, W)], hand.at[:, :, pl.ds(j * B, B)], sem
        ).start()
    pltpu.make_async_copy(hand, hand, sem).wait()


DIMS = (((1,), (1,)), ((), ()))


def factor_of(arrived, inverse, out, parts, panel, sem):
    copy = pltpu.make_async_copy(arrived.at[:, pl.ds(W, 4)], parts, sem)
    copy.start()
    copy.wait()
    for c in range(G):
        for j in range(4):
            part = parts[c, j].astype(jnp.float32)
            panel[:, c * 8:c * 8 + 8, j * B:j * B + B] = part.reshape(W, 8, B)

    @pl.loop(0, W)
    def _(p):
        out[pl.ds(pl.multiple_of(p * B, B), B), :] = lax.dot_general(
            panel[p].astype(jnp.bfloat16), inverse[...], DIMS, preferred_element_type=jnp.float32
        ).astype(jnp.bfloat16)


def keep(inv_ref, inv2_ref, *refs):
    arrived_a, refs = refs[:8], refs[8:]
    arrived_b, rows, inverse, base, kept_a, kept_b, pieces, panel, sem_a, sem_b, sem_p = refs
    sib, row = lax.axis_index("sib"), lax.axis_index("row")

    for step in range(8):
        z = lax.bitwise_and(row // 2 - jnp.where(row % 2 == 0, step, -step), 7)
        for e in range(2):
            origin = z * 2 + lax.bitwise_xor(row % 2, e)
            for h in range(2):
                pltpu.make_async_copy(
                    arrived_a[step].at[e, pl.ds(HA, TAIL), pl.ds(h * PANEL, PANEL)], pieces.at[origin, h], sem_p
                ).start()

    @pl.loop(0, W)
    def _(i):
        for child, ref in enumerate((inv_ref, inv2_ref)):
            e, k = row_landing(ref, i)
            for step in range(8):
                @pl.when(k == step)
                def _():
                    pltpu.make_async_copy(
                        arrived_a[step].at[e, pl.ds(0, HA), pl.ds(child * PANEL, PANEL)], kept_a.at[child, i], sem_a
                    ).start()
    for j in range(W // 2):
        pltpu.make_async_copy(
            arrived_b.at[col_landing(inv_ref, sib, j), pl.ds(0, W)], kept_b.at[:, :, pl.ds(j * B, B)], sem_b
        ).start()
    pltpu.make_async_copy(pieces, pieces, sem_p).wait()
    f32 = jnp.float32
    for p in range(W // 2):
        for r in range(G):
            low = (p % 2) * 8
            panel[p * B + r * 8:p * B + r * 8 + 8, :] = pieces[r, p // 2].astype(f32)[low:low + 8]
    cols = lax.dot_general(panel[...].astype(jnp.bfloat16), inverse[...], DIMS, preferred_element_type=f32)
    panel[...] = cols.astype(jnp.bfloat16).astype(f32)
    pltpu.make_async_copy(kept_a, kept_a, sem_a).wait()
    pltpu.make_async_copy(kept_b, kept_b, sem_b).wait()

    @pl.loop(0, W)
    def _(i):
        block = rows[pl.ds(pl.multiple_of(i * B, B), B), :]
        product = lax.dot_general(block, panel[...].astype(jnp.bfloat16), DIMS, preferred_element_type=f32)
        base[i, 0:HA] = kept_a[0, i].astype(f32) + kept_a[1, i].astype(f32) - product[0:HA]
        base[i, HA:B] = kept_b[i].astype(f32) - product[HA:B]


def join(base, got_b, out):
    out[:, 0:HA] = base[:, 0:HA]
    out[:, HA:B] = base[:, HA:B] + got_b[...].astype(jnp.float32)


def core_exchange(swap):
    return lax.ppermute(swap, "row", [(i, i ^ 1) for i in range(G)])


def pairs_of(own, other):
    return [jnp.stack([own[k], other[k]]) for k in range(8)]


def z_ring(both):
    arrived = [both[0]] + [None] * 7
    for k in (4, 3, 5, 2, 6, 1, 7):
        pairs = [(z * 2 + c, (z + (k if c == 0 else -k)) % 8 * 2 + c) for z in range(8) for c in range(2)]
        arrived[k] = lax.ppermute(both[k], "row", pairs)
    return arrived


def inverse_of(maps):
    blocks = jnp.arange(maps.shape[0], dtype=jnp.int32)
    return jnp.sum(jnp.where(maps[None, :] == blocks[:, None], blocks[None, :], 0), axis=1)


def panel_column(tile, maps):
    mine = lax.dynamic_slice_in_dim(maps, lax.axis_index("col") * W, W, 0)
    owned = jnp.sum(jnp.where(mine < 4, jnp.arange(W, dtype=jnp.int32), 0))
    column = lax.dynamic_slice(tile, (0, owned * B), (W * B, B))
    return jnp.transpose(column.reshape(W, G, 8, B), (1, 0, 2, 3)).reshape(G, W * 8, B)


def panel_slots(got, maps, inv):
    got = jnp.transpose(jnp.take(got, inv[:4] // W, axis=0, mode="clip"), (1, 0, 2, 3))
    targets = lax.dynamic_slice_in_dim(maps, lax.axis_index("row") * W, W, 0) // W
    match = targets[None, :] == (jnp.arange(2 * G, dtype=jnp.int32) % G)[:, None]
    source = jnp.sum(jnp.where(match, jnp.arange(W, dtype=jnp.int32)[None, :], 0), axis=1)
    return jnp.take(got, source, axis=0, mode="clip")


def panel_piece(got, inv, inv2):
    sib, row = lax.axis_index("sib"), lax.axis_index("row")
    slots = [
        child * G + lax.dynamic_slice_in_dim(ref, row * W, W, 0) // W for child, ref in ((sib, inv), (1 - sib, inv2))
    ]
    parts = jnp.take(got, jnp.concatenate(slots), axis=0, mode="clip").astype(jnp.float32)
    return (parts[:W] + parts[W:]).astype(jnp.bfloat16)


def tail_piece(piece):
    sib, row = lax.axis_index("sib"), lax.axis_index("row")
    half = jnp.where(sib == row // 8, 0, 1)
    send = lax.dynamic_slice_in_dim(jnp.transpose(piece, (0, 2, 1, 3)).reshape(W * 8, PANEL), half * (W * 4), W * 4, 0)
    pairs = []
    for s in range(2):
        for g in range(G):
            for c in range(G):
                x = 0 if s == g // 8 else 1
                pairs.append((s * 256 + g * G + c, (g // 8) * 256 + c * G + (g % 8) * 2 + x))
    got = lax.ppermute(send, ("sib", "row", "col"), pairs)
    return jnp.concatenate([got[:16], got[16:]], axis=1)


def shards(children, block_map, inverse_factor):
    tile = children[0]
    maps = block_map[0]
    dma = pltpu.SemaphoreType.DMA
    MiB = 1 << 20
    exchange = [(0, 1), (1, 0)]
    inv = inverse_of(maps)
    blocks = tile.reshape(W, B, W * B)

    rows_a, rows_b = bf16(8, HA, W * B), bf16(8, HB, W * B)
    send_a = pl.pallas_call(
        pack_cols, out_shape=bf16(G, W + 1, HA, B), in_specs=[SMEM, ANY, ANY], out_specs=ANY,
        scratch_shapes=[dma, dma], **params(moved=2 * MiB),
    )(maps, blocks, panel_column(tile, maps))
    own, swap = pl.pallas_call(
        pack_rows, out_shape=(rows_b, rows_b), in_specs=[SMEM, ANY], out_specs=(ANY, ANY), scratch_shapes=[dma],
        **params(moved=2 * MiB),
    )(maps, blocks)
    got_a = lax.all_to_all(send_a, "col", 0, 0, tiled=True)
    other, maps_later = lax.optimization_barrier((core_exchange(swap), maps))
    maps2 = lax.ppermute(maps_later, "sib", exchange)
    got_b = z_ring(pairs_of(own, other))
    got_a, maps2, got_b[7], got_b[6], got_b[5] = lax.optimization_barrier(
        (got_a, maps2, got_b[7], got_b[6], got_b[5]))

    inv2 = inverse_of(maps2)
    pieces, got_a = lax.optimization_barrier((panel_slots(got_a[:, W].reshape(G, W, 8, B), maps, inv), got_a))
    hand_a = pl.pallas_call(
        hand_cols, out_shape=bf16(W, HA, PANEL), in_specs=[SMEM, ANY], out_specs=VMEM, scratch_shapes=[dma],
        **params(moved=MiB),
    )(inv, got_a)
    taken_a = lax.ppermute(hand_a, "sib", exchange)
    send_b = pl.pallas_call(
        rows_to_cols, out_shape=bf16(G, W + 4, HB, B), in_specs=[SMEM, SMEM] + [ANY] * 8, out_specs=ANY,
        scratch_shapes=[dma], **params(moved=2 * MiB),
    )(maps, inv, *got_b)
    pieces = lax.all_to_all(pieces, ("sib", "row"), 0, 0, tiled=True)
    own, swap = pl.pallas_call(
        cols_to_rows, out_shape=(rows_a, rows_a), in_specs=[SMEM] * 3 + [ANY] * 2, out_specs=(ANY, ANY),
        scratch_shapes=[dma], **params(moved=2 * MiB),
    )(maps, maps2, inv, got_a, taken_a)
    pieces, send_b = lax.optimization_barrier((pieces, send_b))
    piece = panel_piece(pieces, inv, inv2)
    tail = tail_piece(piece)
    send_b = pl.pallas_call(
        add_piece, out_shape=bf16(G, W + 4, HB, B), in_specs=[ANY, ANY], out_specs=ANY, scratch_shapes=[dma],
        input_output_aliases={1: 0}, **params(moved=MiB),
    )(jnp.transpose(piece, (1, 0, 2, 3)).reshape(4, W * 8, B), send_b)
    send_b, tail, own, swap = lax.optimization_barrier((send_b, tail, own, swap))
    got_b = lax.all_to_all(send_b, "col", 0, 0, tiled=True)
    other = core_exchange(swap)
    tails = jnp.stack([tail, core_exchange(tail)])
    got_a = z_ring([jnp.concatenate([both, tails], axis=1) for both in pairs_of(own, other)])
    got_b, got_a = lax.optimization_barrier((got_b, got_a))

    hand_b = pl.pallas_call(
        hand_cols, out_shape=bf16(W, HB, PANEL), in_specs=[SMEM, ANY], out_specs=VMEM, scratch_shapes=[dma],
        **params(moved=MiB),
    )(inv, got_b)
    taken_b = lax.ppermute(hand_b, "sib", exchange)
    factor_rows = pl.pallas_call(
        factor_of, out_shape=bf16(W * B, PANEL), in_specs=[ANY, VMEM], out_specs=VMEM,
        scratch_shapes=[pltpu.VMEM((G, 4, W * 8, B), jnp.bfloat16), pltpu.VMEM((W, B, PANEL), jnp.float32), dma],
        **params(flops=2 * W * B * PANEL * PANEL, moved=2 * MiB),
    )(got_b, inverse_factor)
    full = jax.ShapeDtypeStruct((W, B, PANEL), jnp.float32)
    base = pl.pallas_call(
        keep, out_shape=full, in_specs=[SMEM] * 2 + [ANY] * 9 + [VMEM] * 2, out_specs=VMEM,
        scratch_shapes=[pltpu.VMEM((2, W, HA, PANEL), jnp.bfloat16), pltpu.VMEM((W, HB, PANEL), jnp.bfloat16),
                        pltpu.VMEM((G, 2, 16, PANEL), jnp.bfloat16), pltpu.VMEM((PANEL, PANEL), jnp.float32), dma, dma, dma],
        **params(flops=3 * W * B * PANEL * PANEL, moved=6 * MiB),
    )(inv, inv2, *got_a, got_b, factor_rows, inverse_factor)
    full_spec = pl.BlockSpec((2, B, PANEL), lambda i: (i, 0, 0))
    out = pl.pallas_call(
        join, grid=(W // 2,), out_shape=full, in_specs=[full_spec, pl.BlockSpec((2, HB, PANEL), lambda i: (i, 0, 0))],
        out_specs=full_spec, **params(moved=5 * MiB),
    )(base, taken_b)
    return out.reshape(W * B, PANEL)


def solution(mesh):
    in_specs = (P("sib", "row", "col"), P("sib", None), P())
    out_specs = P("row", ("sib", "col"))
    return jax.shard_map(shards, mesh=mesh, in_specs=in_specs, out_specs=out_specs, check_vma=False)
```

```python
import jax
import jax.numpy as jnp
from jax import lax
from jax.experimental import pallas as pl
from jax.experimental.pallas import tpu as pltpu
from jax.sharding import PartitionSpec as P

B = 128
HA = 64
HB = B - HA
W = 8
G = 16
PANEL = 512
TAIL = 16
SMEM = pl.BlockSpec(memory_space=pltpu.SMEM)
ANY = pl.BlockSpec(memory_space=pl.ANY)
VMEM = pl.BlockSpec(memory_space=pltpu.VMEM)
VMEM_LIMIT = 40 * 1024 * 1024


def params(flops=0, moved=0):
    return dict(
        compiler_params=pltpu.CompilerParams(vmem_limit_bytes=VMEM_LIMIT),
        cost_estimate=pl.CostEstimate(flops=flops, bytes_accessed=moved, transcendentals=0),
    )


def bf16(*shape):
    return jax.ShapeDtypeStruct(shape, jnp.bfloat16)


def ring(core, distance):
    return lax.bitwise_and(jnp.where(core == 0, distance, -distance), 7)


def row_slot(map_ref, q):
    row = lax.axis_index("row")
    target = map_ref[row * W + q] // W
    core = target % 2
    return lax.bitwise_xor(core, row % 2), ring(core, target // 2 - row // 2)


def row_landing(inv_ref, i):
    row = lax.axis_index("row")
    source = inv_ref[row * W + i] // W
    return lax.bitwise_xor(source % 2, row % 2), ring(row % 2, row // 2 - source // 2)


def col_slot(map_ref, v):
    return (map_ref[lax.axis_index("col") * W + v] // (W // 2)) % G


def col_landing(inv_ref, half, j):
    return inv_ref[(half * G + lax.axis_index("col")) * (W // 2) + j] // W


def lanes(j):
    return pl.ds(pl.multiple_of(j * B, B), B)


def pack_cols(map_ref, tile, column, a, sem_a, sem_c):
    for v in range(W):
        pltpu.make_async_copy(
            tile.at[:, pl.ds(0, HA), pl.ds(v * B, B)], a.at[col_slot(map_ref, v), pl.ds(0, W)], sem_a
        ).start()
    sixteenths = pltpu.make_async_copy(column, a.at[:, W], sem_c)
    sixteenths.start()
    done = a.at[pl.ds(0, W), pl.ds(0, W)]
    pltpu.make_async_copy(done, done, sem_a).wait()
    sixteenths.wait()


def pack_rows(map_ref, tile, own, swap, sem):
    for q in range(W):
        e, k = row_slot(map_ref, q)
        for side, ob in enumerate((own, swap)):
            @pl.when(e == side)
            def _():
                pltpu.make_async_copy(tile.at[q, pl.ds(HA, HB), :], ob.at[k], sem).start()
    pltpu.make_async_copy(own, own, sem).wait()


def cols_to_rows(map_ref, map2_ref, inv_ref, arrived, taken, own, swap, sem):
    sib = lax.axis_index("sib")

    @pl.loop(0, W)
    def _(q):
        e, k = row_slot(map_ref, q)
        e2, k2 = row_slot(map2_ref, q)
        for side, ob in enumerate((own, swap)):
            @pl.when(e == side)
            def _():
                for j in range(W // 2):
                    pltpu.make_async_copy(
                        arrived.at[col_landing(inv_ref, sib, j), q], ob.at[k, :, pl.ds(j * B, B)], sem
                    ).start()

            @pl.when(e2 == side)
            def _():
                pltpu.make_async_copy(taken.at[q], ob.at[k2, :, pl.ds(PANEL, PANEL)], sem).start()
    pltpu.make_async_copy(own, own, sem).wait()


def rows_to_cols(map_ref, inv_ref, *refs):
    arrived, a, sem = refs[:8], refs[8], refs[9]

    @pl.loop(0, W)
    def _(i):
        e, k = row_landing(inv_ref, i)
        for step in range(8):
            @pl.when(k == step)
            def _():
                for v in range(W):
                    pltpu.make_async_copy(
                        arrived[step].at[e, :, pl.ds(v * B, B)], a.at[col_slot(map_ref, v), i], sem
                    ).start()
    done = a.at[pl.ds(0, W), pl.ds(0, W)]
    pltpu.make_async_copy(done, done, sem).wait()


def add_piece(piece, a, filled, sem):
    for t in range(G):
        pltpu.make_async_copy(piece, filled.at[t, pl.ds(W, 4)], sem).start()
    done = filled.at[:, pl.ds(W, 4)]
    pltpu.make_async_copy(done, done, sem).wait()


def hand_cols(inv_ref, arrived, hand, sem):
    sib = lax.axis_index("sib")
    for j in range(W // 2):
        pltpu.make_async_copy(
            arrived.at[col_landing(inv_ref, 1 - sib, j), pl.ds(0, W)], hand.at[:, :, pl.ds(j * B, B)], sem
        ).start()
    pltpu.make_async_copy(hand, hand, sem).wait()


DIMS = (((1,), (1,)), ((), ()))


def factor_of(arrived, inverse, out, parts, panel, sem):
    copy = pltpu.make_async_copy(arrived.at[:, pl.ds(W, 4)], parts, sem)
    copy.start()
    copy.wait()
    for c in range(G):
        for j in range(4):
            part = parts[c, j].astype(jnp.float32)
            panel[:, c * 8:c * 8 + 8, j * B:j * B + B] = part.reshape(W, 8, B)

    @pl.loop(0, W)
    def _(p):
        out[pl.ds(pl.multiple_of(p * B, B), B), :] = lax.dot_general(
            panel[p].astype(jnp.bfloat16), inverse[...], DIMS, preferred_element_type=jnp.float32
        ).astype(jnp.bfloat16)


def keep(inv_ref, inv2_ref, *refs):
    arrived_a, refs = refs[:8], refs[8:]
    arrived_b, rows, inverse, base, kept_a, kept_b, pieces, panel, sem_a, sem_b, sem_p = refs
    sib, row = lax.axis_index("sib"), lax.axis_index("row")

    for step in range(8):
        z = lax.bitwise_and(row // 2 - jnp.where(row % 2 == 0, step, -step), 7)
        for e in range(2):
            origin = z * 2 + lax.bitwise_xor(row % 2, e)
            for h in range(2):
                pltpu.make_async_copy(
                    arrived_a[step].at[e, pl.ds(HA, TAIL), pl.ds(h * PANEL, PANEL)], pieces.at[origin, h], sem_p
                ).start()

    @pl.loop(0, W)
    def _(i):
        for child, ref in enumerate((inv_ref, inv2_ref)):
            e, k = row_landing(ref, i)
            for step in range(8):
                @pl.when(k == step)
                def _():
                    pltpu.make_async_copy(
                        arrived_a[step].at[e, pl.ds(0, HA), pl.ds(child * PANEL, PANEL)], kept_a.at[child, i], sem_a
                    ).start()
    for j in range(W // 2):
        pltpu.make_async_copy(
            arrived_b.at[col_landing(inv_ref, sib, j), pl.ds(0, W)], kept_b.at[:, :, pl.ds(j * B, B)], sem_b
        ).start()
    pltpu.make_async_copy(pieces, pieces, sem_p).wait()
    f32 = jnp.float32
    for p in range(W // 2):
        for r in range(G):
            low = (p % 2) * 8
            panel[p * B + r * 8:p * B + r * 8 + 8, :] = pieces[r, p // 2].astype(f32)[low:low + 8]
    cols = lax.dot_general(panel[...].astype(jnp.bfloat16), inverse[...], DIMS, preferred_element_type=f32)
    panel[...] = cols.astype(jnp.bfloat16).astype(f32)
    pltpu.make_async_copy(kept_a, kept_a, sem_a).wait()
    pltpu.make_async_copy(kept_b, kept_b, sem_b).wait()

    @pl.loop(0, W)
    def _(i):
        block = rows[pl.ds(pl.multiple_of(i * B, B), B), :]
        product = lax.dot_general(block, panel[...].astype(jnp.bfloat16), DIMS, preferred_element_type=f32)
        base[i, 0:HA] = kept_a[0, i].astype(f32) + kept_a[1, i].astype(f32) - product[0:HA]
        base[i, HA:B] = kept_b[i].astype(f32) - product[HA:B]


def join(base, got_b, out):
    out[:, 0:HA] = base[:, 0:HA]
    out[:, HA:B] = base[:, HA:B] + got_b[...].astype(jnp.float32)


def core_exchange(swap):
    return lax.ppermute(swap, "row", [(i, i ^ 1) for i in range(G)])


def pairs_of(own, other):
    return [jnp.stack([own[k], other[k]]) for k in range(8)]


def z_ring(both):
    arrived = [both[0]] + [None] * 7
    for k in (4, 3, 5, 2, 6, 1, 7):
        pairs = [(z * 2 + c, (z + (k if c == 0 else -k)) % 8 * 2 + c) for z in range(8) for c in range(2)]
        arrived[k] = lax.ppermute(both[k], "row", pairs)
    return arrived


def inverse_of(maps):
    blocks = jnp.arange(maps.shape[0], dtype=jnp.int32)
    return jnp.sum(jnp.where(maps[None, :] == blocks[:, None], blocks[None, :], 0), axis=1)


def panel_column(tile, maps):
    mine = lax.dynamic_slice_in_dim(maps, lax.axis_index("col") * W, W, 0)
    owned = jnp.sum(jnp.where(mine < 4, jnp.arange(W, dtype=jnp.int32), 0))
    column = lax.dynamic_slice(tile, (0, owned * B), (W * B, B))
    return jnp.transpose(column.reshape(W, G, 8, B), (1, 0, 2, 3)).reshape(G, W * 8, B)


def panel_slots(got, maps, inv):
    got = jnp.transpose(jnp.take(got, inv[:4] // W, axis=0, mode="clip"), (1, 0, 2, 3))
    targets = lax.dynamic_slice_in_dim(maps, lax.axis_index("row") * W, W, 0) // W
    match = targets[None, :] == (jnp.arange(2 * G, dtype=jnp.int32) % G)[:, None]
    source = jnp.sum(jnp.where(match, jnp.arange(W, dtype=jnp.int32)[None, :], 0), axis=1)
    return jnp.take(got, source, axis=0, mode="clip")


def panel_piece(got, inv, inv2):
    sib, row = lax.axis_index("sib"), lax.axis_index("row")
    slots = [
        child * G + lax.dynamic_slice_in_dim(ref, row * W, W, 0) // W for child, ref in ((sib, inv), (1 - sib, inv2))
    ]
    parts = jnp.take(got, jnp.concatenate(slots), axis=0, mode="clip").astype(jnp.float32)
    return (parts[:W] + parts[W:]).astype(jnp.bfloat16)


def tail_piece(piece):
    sib, row = lax.axis_index("sib"), lax.axis_index("row")
    half = jnp.where(sib == row // 8, 0, 1)
    send = lax.dynamic_slice_in_dim(jnp.transpose(piece, (0, 2, 1, 3)).reshape(W * 8, PANEL), half * (W * 4), W * 4, 0)
    pairs = []
    for s in range(2):
        for g in range(G):
            for c in range(G):
                x = 0 if s == g // 8 else 1
                pairs.append((s * 256 + g * G + c, (g // 8) * 256 + c * G + (g % 8) * 2 + x))
    got = lax.ppermute(send, ("sib", "row", "col"), pairs)
    return jnp.concatenate([got[:16], got[16:]], axis=1)


def shards(children, block_map, inverse_factor):
    tile = children[0]
    maps = block_map[0]
    dma = pltpu.SemaphoreType.DMA
    MiB = 1 << 20
    exchange = [(0, 1), (1, 0)]
    inv = inverse_of(maps)
    blocks = tile.reshape(W, B, W * B)

    rows_a, rows_b = bf16(8, HA, W * B), bf16(8, HB, W * B)
    send_a = pl.pallas_call(
        pack_cols, out_shape=pltpu.HBM((G, W + 1, HA, B), jnp.bfloat16), in_specs=[SMEM, ANY, ANY], out_specs=ANY,
        scratch_shapes=[dma, dma], **params(moved=2 * MiB),
    )(maps, blocks, panel_column(tile, maps))
    own, swap = pl.pallas_call(
        pack_rows, out_shape=(rows_b, rows_b), in_specs=[SMEM, ANY], out_specs=(ANY, ANY), scratch_shapes=[dma],
        **params(moved=2 * MiB),
    )(maps, blocks)
    got_a = lax.all_to_all(send_a, "col", 0, 0, tiled=True)
    other, maps_later = lax.optimization_barrier((core_exchange(swap), maps))
    maps2 = lax.ppermute(maps_later, "sib", exchange)
    got_b = z_ring(pairs_of(own, other))
    got_a, maps2, got_b[7], got_b[6] = lax.optimization_barrier((got_a, maps2, got_b[7], got_b[6]))

    inv2 = inverse_of(maps2)
    pieces, got_a = lax.optimization_barrier((panel_slots(got_a[:, W].reshape(G, W, 8, B), maps, inv), got_a))
    hand_a = pl.pallas_call(
        hand_cols, out_shape=bf16(W, HA, PANEL), in_specs=[SMEM, ANY], out_specs=VMEM, scratch_shapes=[dma],
        **params(moved=MiB),
    )(inv, got_a)
    taken_a = lax.ppermute(hand_a, "sib", exchange)
    send_b = pl.pallas_call(
        rows_to_cols, out_shape=bf16(G, W + 4, HB, B), in_specs=[SMEM, SMEM] + [ANY] * 8, out_specs=ANY,
        scratch_shapes=[dma], **params(moved=2 * MiB),
    )(maps, inv, *got_b)
    pieces = lax.all_to_all(pieces, ("sib", "row"), 0, 0, tiled=True)
    own, swap = pl.pallas_call(
        cols_to_rows, out_shape=(rows_a, rows_a), in_specs=[SMEM] * 3 + [ANY] * 2, out_specs=(ANY, ANY),
        scratch_shapes=[dma], **params(moved=2 * MiB),
    )(maps, maps2, inv, got_a, taken_a)
    pieces, send_b = lax.optimization_barrier((pieces, send_b))
    piece = panel_piece(pieces, inv, inv2)
    tail = tail_piece(piece)
    send_b = pl.pallas_call(
        add_piece, out_shape=bf16(G, W + 4, HB, B), in_specs=[ANY, ANY], out_specs=ANY, scratch_shapes=[dma],
        input_output_aliases={1: 0}, **params(moved=MiB),
    )(jnp.transpose(piece, (1, 0, 2, 3)).reshape(4, W * 8, B), send_b)
    send_b, tail, own, swap = lax.optimization_barrier((send_b, tail, own, swap))
    got_b = lax.all_to_all(send_b, "col", 0, 0, tiled=True)
    other = core_exchange(swap)
    tails = jnp.stack([tail, core_exchange(tail)])
    got_a = z_ring([jnp.concatenate([both, tails], axis=1) for both in pairs_of(own, other)])
    got_b, got_a = lax.optimization_barrier((got_b, got_a))

    hand_b = pl.pallas_call(
        hand_cols, out_shape=bf16(W, HB, PANEL), in_specs=[SMEM, ANY], out_specs=VMEM, scratch_shapes=[dma],
        **params(moved=MiB),
    )(inv, got_b)
    taken_b = lax.ppermute(hand_b, "sib", exchange)
    factor_rows = pl.pallas_call(
        factor_of, out_shape=bf16(W * B, PANEL), in_specs=[ANY, VMEM], out_specs=VMEM,
        scratch_shapes=[pltpu.VMEM((G, 4, W * 8, B), jnp.bfloat16), pltpu.VMEM((W, B, PANEL), jnp.float32), dma],
        **params(flops=2 * W * B * PANEL * PANEL, moved=2 * MiB),
    )(got_b, inverse_factor)
    full = jax.ShapeDtypeStruct((W, B, PANEL), jnp.float32)
    base = pl.pallas_call(
        keep, out_shape=full, in_specs=[SMEM] * 2 + [ANY] * 9 + [VMEM] * 2, out_specs=VMEM,
        scratch_shapes=[pltpu.VMEM((2, W, HA, PANEL), jnp.bfloat16), pltpu.VMEM((W, HB, PANEL), jnp.bfloat16),
                        pltpu.VMEM((G, 2, 16, PANEL), jnp.bfloat16), pltpu.VMEM((PANEL, PANEL), jnp.float32), dma, dma, dma],
        **params(flops=3 * W * B * PANEL * PANEL, moved=6 * MiB),
    )(inv, inv2, *got_a, got_b, factor_rows, inverse_factor)
    full_spec = pl.BlockSpec((2, B, PANEL), lambda i: (i, 0, 0))
    out = pl.pallas_call(
        join, grid=(W // 2,), out_shape=full, in_specs=[full_spec, pl.BlockSpec((2, HB, PANEL), lambda i: (i, 0, 0))],
        out_specs=full_spec, **params(moved=5 * MiB),
    )(base, taken_b)
    return out.reshape(W * B, PANEL)


def solution(mesh):
    in_specs = (P("sib", "row", "col"), P("sib", None), P())
    out_specs = P("row", ("sib", "col"))
    return jax.shard_map(shards, mesh=mesh, in_specs=in_specs, out_specs=out_specs, check_vma=False)
```

```python
import jax
import jax.numpy as jnp
from jax import lax
from jax.experimental import pallas as pl
from jax.experimental.pallas import tpu as pltpu
from jax.sharding import PartitionSpec as P

B = 128
HA = 64
HB = B - HA
W = 8
G = 16
PANEL = 512
TAIL = 16
SMEM = pl.BlockSpec(memory_space=pltpu.SMEM)
ANY = pl.BlockSpec(memory_space=pl.ANY)
VMEM = pl.BlockSpec(memory_space=pltpu.VMEM)
VMEM_LIMIT = 40 * 1024 * 1024


def params(flops=0, moved=0):
    return dict(
        compiler_params=pltpu.CompilerParams(vmem_limit_bytes=VMEM_LIMIT),
        cost_estimate=pl.CostEstimate(flops=flops, bytes_accessed=moved, transcendentals=0),
    )


def bf16(*shape):
    return jax.ShapeDtypeStruct(shape, jnp.bfloat16)


def ring(core, distance):
    return lax.bitwise_and(jnp.where(core == 0, distance, -distance), 7)


def row_slot(map_ref, q):
    row = lax.axis_index("row")
    target = map_ref[row * W + q] // W
    core = target % 2
    return lax.bitwise_xor(core, row % 2), ring(core, target // 2 - row // 2)


def row_landing(inv_ref, i):
    row = lax.axis_index("row")
    source = inv_ref[row * W + i] // W
    return lax.bitwise_xor(source % 2, row % 2), ring(row % 2, row // 2 - source // 2)


def col_slot(map_ref, v):
    return (map_ref[lax.axis_index("col") * W + v] // (W // 2)) % G


def col_landing(inv_ref, half, j):
    return inv_ref[(half * G + lax.axis_index("col")) * (W // 2) + j] // W


def lanes(j):
    return pl.ds(pl.multiple_of(j * B, B), B)


def pack_cols(map_ref, tile, column, a, sem_a, sem_c):
    for v in range(W):
        pltpu.make_async_copy(
            tile.at[:, pl.ds(0, HA), pl.ds(v * B, B)], a.at[col_slot(map_ref, v), pl.ds(0, W)], sem_a
        ).start()
    sixteenths = pltpu.make_async_copy(column, a.at[:, W], sem_c)
    sixteenths.start()
    done = a.at[pl.ds(0, W), pl.ds(0, W)]
    pltpu.make_async_copy(done, done, sem_a).wait()
    sixteenths.wait()


def pack_rows(map_ref, tile, own, swap, sem):
    for q in range(W):
        e, k = row_slot(map_ref, q)
        for side, ob in enumerate((own, swap)):
            @pl.when(e == side)
            def _():
                pltpu.make_async_copy(tile.at[q, pl.ds(HA, HB), :], ob.at[k], sem).start()
    pltpu.make_async_copy(own, own, sem).wait()


def cols_to_rows(map_ref, map2_ref, inv_ref, arrived, taken, own, swap, sem):
    sib = lax.axis_index("sib")

    @pl.loop(0, W)
    def _(q):
        e, k = row_slot(map_ref, q)
        e2, k2 = row_slot(map2_ref, q)
        for side, ob in enumerate((own, swap)):
            @pl.when(e == side)
            def _():
                for j in range(W // 2):
                    pltpu.make_async_copy(
                        arrived.at[col_landing(inv_ref, sib, j), q], ob.at[k, :, pl.ds(j * B, B)], sem
                    ).start()

            @pl.when(e2 == side)
            def _():
                pltpu.make_async_copy(taken.at[q], ob.at[k2, :, pl.ds(PANEL, PANEL)], sem).start()
    pltpu.make_async_copy(own, own, sem).wait()


def rows_to_cols(map_ref, inv_ref, *refs):
    arrived, a, sem = refs[:8], refs[8], refs[9]

    @pl.loop(0, W)
    def _(i):
        e, k = row_landing(inv_ref, i)
        for step in range(8):
            @pl.when(k == step)
            def _():
                for v in range(W):
                    pltpu.make_async_copy(
                        arrived[step].at[e, :, pl.ds(v * B, B)], a.at[col_slot(map_ref, v), i], sem
                    ).start()
    done = a.at[pl.ds(0, W), pl.ds(0, W)]
    pltpu.make_async_copy(done, done, sem).wait()


def add_piece(piece, a, filled, sem):
    for t in range(G):
        pltpu.make_async_copy(piece, filled.at[t, pl.ds(W, 4)], sem).start()
    done = filled.at[:, pl.ds(W, 4)]
    pltpu.make_async_copy(done, done, sem).wait()


def hand_cols(inv_ref, arrived, hand, sem):
    sib = lax.axis_index("sib")
    for j in range(W // 2):
        pltpu.make_async_copy(
            arrived.at[col_landing(inv_ref, 1 - sib, j), pl.ds(0, W)], hand.at[:, :, pl.ds(j * B, B)], sem
        ).start()
    pltpu.make_async_copy(hand, hand, sem).wait()


DIMS = (((1,), (1,)), ((), ()))


def factor_of(arrived, inverse, out, parts, panel, sem):
    copy = pltpu.make_async_copy(arrived.at[:, pl.ds(W, 4)], parts, sem)
    copy.start()
    copy.wait()
    for c in range(G):
        for j in range(4):
            part = parts[c, j].astype(jnp.float32)
            panel[:, c * 8:c * 8 + 8, j * B:j * B + B] = part.reshape(W, 8, B)

    @pl.loop(0, W)
    def _(p):
        out[pl.ds(pl.multiple_of(p * B, B), B), :] = lax.dot_general(
            panel[p].astype(jnp.bfloat16), inverse[...], DIMS, preferred_element_type=jnp.float32
        ).astype(jnp.bfloat16)


def keep(inv_ref, inv2_ref, *refs):
    arrived_a, refs = refs[:8], refs[8:]
    arrived_b, rows, inverse, base, kept_a, kept_b, pieces, panel, sem_a, sem_b, sem_p = refs
    sib, row = lax.axis_index("sib"), lax.axis_index("row")

    for step in range(8):
        z = lax.bitwise_and(row // 2 - jnp.where(row % 2 == 0, step, -step), 7)
        for e in range(2):
            origin = z * 2 + lax.bitwise_xor(row % 2, e)
            for h in range(2):
                pltpu.make_async_copy(
                    arrived_a[step].at[e, pl.ds(HA, TAIL), pl.ds(h * PANEL, PANEL)], pieces.at[origin, h], sem_p
                ).start()

    @pl.loop(0, W)
    def _(i):
        for child, ref in enumerate((inv_ref, inv2_ref)):
            e, k = row_landing(ref, i)
            for step in range(8):
                @pl.when(k == step)
                def _():
                    pltpu.make_async_copy(
                        arrived_a[step].at[e, pl.ds(0, HA), pl.ds(child * PANEL, PANEL)], kept_a.at[child, i], sem_a
                    ).start()
    for j in range(W // 2):
        pltpu.make_async_copy(
            arrived_b.at[col_landing(inv_ref, sib, j), pl.ds(0, W)], kept_b.at[:, :, pl.ds(j * B, B)], sem_b
        ).start()
    pltpu.make_async_copy(pieces, pieces, sem_p).wait()
    f32 = jnp.float32
    for p in range(W // 2):
        for r in range(G):
            low = (p % 2) * 8
            panel[p * B + r * 8:p * B + r * 8 + 8, :] = pieces[r, p // 2].astype(f32)[low:low + 8]
    cols = lax.dot_general(panel[...].astype(jnp.bfloat16), inverse[...], DIMS, preferred_element_type=f32)
    panel[...] = cols.astype(jnp.bfloat16).astype(f32)
    pltpu.make_async_copy(kept_a, kept_a, sem_a).wait()
    pltpu.make_async_copy(kept_b, kept_b, sem_b).wait()

    @pl.loop(0, W)
    def _(i):
        block = rows[pl.ds(pl.multiple_of(i * B, B), B), :]
        product = lax.dot_general(block, panel[...].astype(jnp.bfloat16), DIMS, preferred_element_type=f32)
        base[i, 0:HA] = kept_a[0, i].astype(f32) + kept_a[1, i].astype(f32) - product[0:HA]
        base[i, HA:B] = kept_b[i].astype(f32) - product[HA:B]


def join(base, got_b, out):
    out[:, 0:HA] = base[:, 0:HA]
    out[:, HA:B] = base[:, HA:B] + got_b[...].astype(jnp.float32)


def core_exchange(swap):
    return lax.ppermute(swap, "row", [(i, i ^ 1) for i in range(G)])


def pairs_of(own, other):
    return [jnp.stack([own[k], other[k]]) for k in range(8)]


def z_ring(both):
    arrived = [both[0]] + [None] * 7
    for k in (4, 3, 5, 2, 6, 1, 7):
        pairs = [(z * 2 + c, (z + (k if c == 0 else -k)) % 8 * 2 + c) for z in range(8) for c in range(2)]
        arrived[k] = lax.ppermute(both[k], "row", pairs)
    return arrived


def inverse_of(maps):
    blocks = jnp.arange(maps.shape[0], dtype=jnp.int32)
    return jnp.sum(jnp.where(maps[None, :] == blocks[:, None], blocks[None, :], 0), axis=1)


def panel_column(tile, maps):
    mine = lax.dynamic_slice_in_dim(maps, lax.axis_index("col") * W, W, 0)
    owned = jnp.sum(jnp.where(mine < 4, jnp.arange(W, dtype=jnp.int32), 0))
    column = lax.dynamic_slice(tile, (0, owned * B), (W * B, B))
    return jnp.transpose(column.reshape(W, G, 8, B), (1, 0, 2, 3)).reshape(G, W * 8, B)


def panel_slots(got, maps, inv):
    got = jnp.transpose(jnp.take(got, inv[:4] // W, axis=0, mode="clip"), (1, 0, 2, 3))
    targets = lax.dynamic_slice_in_dim(maps, lax.axis_index("row") * W, W, 0) // W
    match = targets[None, :] == (jnp.arange(2 * G, dtype=jnp.int32) % G)[:, None]
    source = jnp.sum(jnp.where(match, jnp.arange(W, dtype=jnp.int32)[None, :], 0), axis=1)
    return jnp.take(got, source, axis=0, mode="clip")


def panel_piece(got, inv, inv2):
    sib, row = lax.axis_index("sib"), lax.axis_index("row")
    slots = [
        child * G + lax.dynamic_slice_in_dim(ref, row * W, W, 0) // W for child, ref in ((sib, inv), (1 - sib, inv2))
    ]
    parts = jnp.take(got, jnp.concatenate(slots), axis=0, mode="clip").astype(jnp.float32)
    return (parts[:W] + parts[W:]).astype(jnp.bfloat16)


def tail_piece(piece):
    sib, row = lax.axis_index("sib"), lax.axis_index("row")
    half = jnp.where(sib == row // 8, 0, 1)
    send = lax.dynamic_slice_in_dim(jnp.transpose(piece, (0, 2, 1, 3)).reshape(W * 8, PANEL), half * (W * 4), W * 4, 0)
    pairs = []
    for s in range(2):
        for g in range(G):
            for c in range(G):
                x = 0 if s == g // 8 else 1
                pairs.append((s * 256 + g * G + c, (g // 8) * 256 + c * G + (g % 8) * 2 + x))
    got = lax.ppermute(send, ("sib", "row", "col"), pairs)
    return jnp.concatenate([got[:16], got[16:]], axis=1)


def shards(children, block_map, inverse_factor):
    tile = children[0]
    maps = block_map[0]
    dma = pltpu.SemaphoreType.DMA
    MiB = 1 << 20
    exchange = [(0, 1), (1, 0)]
    inv = inverse_of(maps)
    blocks = tile.reshape(W, B, W * B)

    rows_a, rows_b = bf16(8, HA, W * B), bf16(8, HB, W * B)
    send_a = pl.pallas_call(
        pack_cols, out_shape=pltpu.HBM((G, W + 1, HA, B), jnp.bfloat16), in_specs=[SMEM, ANY, ANY], out_specs=ANY,
        scratch_shapes=[dma, dma], **params(moved=2 * MiB),
    )(maps, blocks, panel_column(tile, maps))
    own, swap = pl.pallas_call(
        pack_rows, out_shape=(rows_b, rows_b), in_specs=[SMEM, ANY], out_specs=(ANY, ANY), scratch_shapes=[dma],
        **params(moved=2 * MiB),
    )(maps, blocks)
    got_a = lax.all_to_all(send_a, "col", 0, 0, tiled=True)
    other, maps_later = lax.optimization_barrier((core_exchange(swap), maps))
    maps2 = lax.ppermute(maps_later, "sib", exchange)
    got_b = z_ring(pairs_of(own, other))
    got_a, maps2, got_b[7], got_b[6], got_b[5] = lax.optimization_barrier(
        (got_a, maps2, got_b[7], got_b[6], got_b[5]))

    inv2 = inverse_of(maps2)
    pieces, got_a = lax.optimization_barrier((panel_slots(got_a[:, W].reshape(G, W, 8, B), maps, inv), got_a))
    hand_a = pl.pallas_call(
        hand_cols, out_shape=bf16(W, HA, PANEL), in_specs=[SMEM, ANY], out_specs=VMEM, scratch_shapes=[dma],
        **params(moved=MiB),
    )(inv, got_a)
    taken_a = lax.ppermute(hand_a, "sib", exchange)
    send_b = pl.pallas_call(
        rows_to_cols, out_shape=bf16(G, W + 4, HB, B), in_specs=[SMEM, SMEM] + [ANY] * 8, out_specs=ANY,
        scratch_shapes=[dma], **params(moved=2 * MiB),
    )(maps, inv, *got_b)
    pieces = lax.all_to_all(pieces, ("sib", "row"), 0, 0, tiled=True)
    own, swap = pl.pallas_call(
        cols_to_rows, out_shape=(rows_a, rows_a), in_specs=[SMEM] * 3 + [ANY] * 2, out_specs=(ANY, ANY),
        scratch_shapes=[dma], **params(moved=2 * MiB),
    )(maps, maps2, inv, got_a, taken_a)
    pieces, send_b = lax.optimization_barrier((pieces, send_b))
    piece = panel_piece(pieces, inv, inv2)
    tail = tail_piece(piece)
    send_b = pl.pallas_call(
        add_piece, out_shape=bf16(G, W + 4, HB, B), in_specs=[ANY, ANY], out_specs=ANY, scratch_shapes=[dma],
        input_output_aliases={1: 0}, **params(moved=MiB),
    )(jnp.transpose(piece, (1, 0, 2, 3)).reshape(4, W * 8, B), send_b)
    send_b, tail, own, swap = lax.optimization_barrier((send_b, tail, own, swap))
    got_b = lax.all_to_all(send_b, "col", 0, 0, tiled=True)
    other = core_exchange(swap)
    tails = jnp.stack([tail, core_exchange(tail)])
    got_a = z_ring([jnp.concatenate([both, tails], axis=1) for both in pairs_of(own, other)])
    got_b, got_a = lax.optimization_barrier((got_b, got_a))

    hand_b = pl.pallas_call(
        hand_cols, out_shape=bf16(W, HB, PANEL), in_specs=[SMEM, ANY], out_specs=VMEM, scratch_shapes=[dma],
        **params(moved=MiB),
    )(inv, got_b)
    taken_b = lax.ppermute(hand_b, "sib", exchange)
    factor_rows = pl.pallas_call(
        factor_of, out_shape=bf16(W * B, PANEL), in_specs=[ANY, VMEM], out_specs=VMEM,
        scratch_shapes=[pltpu.VMEM((G, 4, W * 8, B), jnp.bfloat16), pltpu.VMEM((W, B, PANEL), jnp.float32), dma],
        **params(flops=2 * W * B * PANEL * PANEL, moved=2 * MiB),
    )(got_b, inverse_factor)
    full = jax.ShapeDtypeStruct((W, B, PANEL), jnp.float32)
    base = pl.pallas_call(
        keep, out_shape=full, in_specs=[SMEM] * 2 + [ANY] * 9 + [VMEM] * 2, out_specs=VMEM,
        scratch_shapes=[pltpu.VMEM((2, W, HA, PANEL), jnp.bfloat16), pltpu.VMEM((W, HB, PANEL), jnp.bfloat16),
                        pltpu.VMEM((G, 2, 16, PANEL), jnp.bfloat16), pltpu.VMEM((PANEL, PANEL), jnp.float32), dma, dma, dma],
        **params(flops=3 * W * B * PANEL * PANEL, moved=6 * MiB),
    )(inv, inv2, *got_a, got_b, factor_rows, inverse_factor)
    full_spec = pl.BlockSpec((2, B, PANEL), lambda i: (i, 0, 0))
    out = pl.pallas_call(
        join, grid=(W // 2,), out_shape=full, in_specs=[full_spec, pl.BlockSpec((2, HB, PANEL), lambda i: (i, 0, 0))],
        out_specs=full_spec, **params(moved=5 * MiB),
    )(base, taken_b)
    return out.reshape(W * B, PANEL)


def solution(mesh):
    in_specs = (P("sib", "row", "col"), P("sib", None), P())
    out_specs = P("row", ("sib", "col"))
    return jax.shard_map(shards, mesh=mesh, in_specs=in_specs, out_specs=out_specs, check_vma=False)
```
